32 devices in a mesh: groups: 2 (over x), lon: 16 (over z, y, core).
Axes of the slice: x: 2, y: 2, z: 4, core: 2. Of those that a mesh axis runs over, the one named last changes fastest.
Arguments:
- atm_in: bfloat16 [256, 48, 640], P(('groups', 'lon')), parts along dimension 0, may hold values from -6 to 6
- ocean_in: bfloat16 [512, 95, 128], P(('groups', 'lon')), parts along dimension 0, may hold values from -6 to 6
- lift_weight: bfloat16 [48, 256], replicated, may hold values from -0.875 to 0.875
- conv_weight: bfloat16 [3, 3, 256, 256], replicated, may hold values from -0.125 to 0.125
- flux_weight: bfloat16 [256, 16], replicated, may hold values from -0.375 to 0.375
- ocean_weight: bfloat16 [95, 256], replicated, may hold values from -0.625 to 0.625
- couple_weight: bfloat16 [16, 256], replicated, may hold values from -3 to 3
- mix_weight: bfloat16 [256, 256], replicated, may hold values from -0.375 to 0.375
- regrid_weight: bfloat16 [256, 4, 128, 128], P('lon'), may hold values from 0 to 1, as said below
- pair_tile: int32 [256, 3], P('lon'), may hold values from 0 to 39, as said below
- ocean_mask: int32 [256], P('lon'), may hold values from 0 to 1, as said below
Outputs:
- atm_hidden: bfloat16 [256, 256, 640], P(('groups', 'lon')), parts along dimension 0
- ocean_hidden: bfloat16 [512, 256, 128], P(('groups', 'lon')), parts along dimension 0
The draws below stay inside these ranges and needn't reach their ends.
There are 2 independent parts, one for each index of `groups`. The reference program is written for one: setup_inputs(seed, part) draws one part's arguments, and reference() takes and returns one part's arrays. A program takes and returns all parts, laid end to end along the dimension named above; an argument that names none is the same for every part. Nothing has to cross between parts.
Inputs may be any that keep to these rules, and one draw needn't show every extreme that they name: `regrid_weight`: block p = 3 is zero except for the northernmost 2 tiles of each strip (local index 14 and above); blocks 0 to 2 are positive. `pair_tile`: within one of the band of the ocean tile's latitude; column 1 is the band itself. `ocean_mask`: each device's 16 tiles hold between 2 and 8 ones, its northernmost 2 tiles always among them; some device has exactly 8.
All inputs are finite; a program needn't handle non-finite values.
Results may differ from the reference program's by a relative error of at most 0.0053.
Values may be sent and summed in bfloat16 or wider, within the bound.
A program may use at most 128 MiB of HBM per device.

```python
import jax
import jax.numpy as jnp
from jax import lax

ACH = 48
OCH = 95
WIDTH = 256
FLUX = 16
PAIRS = 4
FOLDB = 2
ALON = 8
LAT = 640
TLAT = 16
OT = 16
MAXACT = 8
LONS = 16
AT = 40
TA = 128
TO = 128
NLON = 128
OTILES = 256


def ocean_layout(key):
    base_key = jax.random.fold_in(key, 11)
    key_counts, key_full, key_chosen, key_score = jax.random.split(base_key, 4)
    lowest = max(FOLDB, MAXACT // 4)
    counts = jax.random.randint(key_counts, (LONS,), lowest, MAXACT // 2 + 1)
    full = jax.random.randint(key_full, (LONS,), 0, 8) == 0
    chosen = jax.random.randint(key_chosen, (), 0, LONS)
    full = full | (jnp.arange(LONS) == chosen)
    counts = jnp.where(full, MAXACT, counts).astype(jnp.int32)
    local = jnp.arange(OT, dtype=jnp.int32)
    score = jax.random.randint(key_score, (LONS, OT), 0, 2 ** 20) * OT + local[None, :]
    score = jnp.where(local[None, :] >= OT - FOLDB, local[None, :] - OT, score)
    ranks = jnp.argsort(jnp.argsort(score, axis=1), axis=1)
    water = (ranks < counts[:, None]).astype(jnp.int32)
    return water


def draw_ocean_mask(key, part):
    return ocean_layout(key).reshape(-1)


def draw_pair_tile(key, part):
    bands = jnp.arange(OTILES, dtype=jnp.int32) % OT
    center = jnp.minimum(bands * AT // (OT - 1), AT - 1)
    offsets = jax.random.randint(jax.random.fold_in(key, 5), (OTILES, 3), -1, 2)
    offsets = jnp.where(jnp.arange(3)[None, :] == 1, 0, offsets)
    return jnp.clip(center[:, None] + offsets, 0, AT - 1).astype(jnp.int32)


def draw_regrid_weight(key, part):
    uniform_part = jax.random.uniform(jax.random.fold_in(key, 3), (OTILES, PAIRS, TO, TA), jnp.float32)
    values = jnp.exp(jnp.log(0.01) + uniform_part * jnp.log(100.0))
    bands = jnp.arange(OTILES) % OT
    near_fold = bands >= OT - FOLDB
    last_pair = jnp.arange(PAIRS) == PAIRS - 1
    keep = jnp.where(last_pair[None, :] & jnp.logical_not(near_fold)[:, None], 0.0, 1.0)
    return (values * keep[:, :, None, None]).astype(jnp.bfloat16)


def shard_levels(own_key, dims, cuts, smallest, high):
    def one(position, blocks):
        steps = jax.random.uniform(jax.random.fold_in(jax.random.fold_in(own_key, 6), position), (blocks,), jnp.float32, smallest / len(cuts), high / len(cuts))
        return jnp.repeat(jnp.exp(steps), dims[position] // blocks).reshape((-1,) + (1,) * (len(dims) - position - 1))

    loudness = one(*cuts[0])
    for cut in cuts[1:]:
        loudness = loudness * one(*cut)
    return loudness


def noise(own_key, extent, spread, limit, cuts=(), kind=jnp.bfloat16):
    level = shard_levels(own_key, extent, cuts, -0.22, 0.18) if cuts else 1.0
    array = jax.random.normal(own_key, extent, jnp.float32) * spread * level
    return jnp.minimum(jnp.maximum(array, -limit), limit).astype(kind)


def setup_inputs(seed: int = 0, part: int = 0) -> dict:
    arg_keys = jax.random.split(jax.random.key(seed), 12)
    part_splits = jax.random.split(jax.random.fold_in(arg_keys[11], part), 12)
    return {
        "atm_in": noise(part_splits[0], (NLON, ACH, LAT), 1.0, 6.0, ((0, 16),)),
        "ocean_in": noise(part_splits[1], (OTILES, OCH, TO), 1.0, 6.0, ((0, 16),)),
        "lift_weight": noise(arg_keys[2], (ACH, WIDTH), ACH ** -0.5, 0.875),
        "conv_weight": noise(arg_keys[3], (3, 3, WIDTH, WIDTH), (9 * WIDTH) ** -0.5, 0.125),
        "flux_weight": noise(arg_keys[4], (WIDTH, FLUX), WIDTH ** -0.5, 0.375),
        "ocean_weight": noise(arg_keys[5], (OCH, WIDTH), OCH ** -0.5, 0.625),
        "couple_weight": noise(arg_keys[6], (FLUX, WIDTH), (FLUX // 4) ** -0.5, 3.0),
        "mix_weight": noise(arg_keys[7], (WIDTH, WIDTH), WIDTH ** -0.5, 0.375),
        "regrid_weight": draw_regrid_weight(jax.random.fold_in(arg_keys[11], 71), part),
        "pair_tile": draw_pair_tile(jax.random.fold_in(arg_keys[11], 71), part),
        "ocean_mask": draw_ocean_mask(jax.random.fold_in(arg_keys[11], 71), part),
    }


def reference(atm_in, ocean_in, lift_weight, conv_weight, flux_weight, ocean_weight, couple_weight, mix_weight, regrid_weight, pair_tile, ocean_mask):
    single = jnp.float32
    lifted = jnp.einsum('xcy,co->xoy', atm_in.astype(single), lift_weight.astype(single)).astype(jnp.bfloat16)
    wrapped = jnp.concatenate([lifted[-1:], lifted, lifted[:1]], 0)
    wrapped = jnp.pad(wrapped, ((0, 0), (0, 0), (1, 1)))
    taps = conv_weight.astype(single)

    def conv_block(index):
        slab_part = lax.dynamic_slice_in_dim(wrapped, (index * ALON).astype(jnp.int32), ALON + 2, 0).astype(single)
        total = jnp.zeros((ALON, WIDTH, LAT), single)
        for shift_x in range(3):
            for shift_y in range(3):
                total = total + jnp.einsum('xcy,co->xoy', slab_part[shift_x:shift_x + ALON, :, shift_y:shift_y + LAT], taps[shift_x, shift_y])
        return total

    conv = lax.map(conv_block, jnp.arange(LONS, dtype=jnp.int32)).reshape(NLON, WIDTH, LAT)
    atm_hidden = (lifted.astype(single) + jax.nn.gelu(conv)).astype(jnp.bfloat16)
    flux = jnp.einsum('xhy,hf->xfy', atm_hidden.astype(single), flux_weight.astype(single)).astype(jnp.bfloat16)
    flux_tile = flux.reshape(LONS, ALON, FLUX, AT, TLAT).transpose(0, 3, 2, 1, 4).reshape(LONS, AT, FLUX, TA)

    def ocean_device(device):
        west = jnp.mod(device - 1 + LONS, LONS).astype(jnp.int32)
        east = jnp.mod(device + 1, LONS).astype(jnp.int32)
        mirror = (LONS - 1 - device).astype(jnp.int32)
        table = jnp.concatenate([flux_tile[west], flux_tile[device], flux_tile[east], flux_tile[mirror, AT - 1][None]], 0)
        start = (device * OT).astype(jnp.int32)
        states = lax.dynamic_slice_in_dim(ocean_in, start, OT, 0).astype(single)
        blocks = lax.dynamic_slice_in_dim(regrid_weight, start, OT, 0).astype(single)
        bands = lax.dynamic_slice_in_dim(pair_tile, start, OT, 0)
        water = lax.dynamic_slice_in_dim(ocean_mask, start, OT, 0)
        index = jnp.concatenate([bands + jnp.arange(3, dtype=jnp.int32)[None, :] * AT, jnp.full((OT, 1), 3 * AT, jnp.int32)], 1)
        got = table[index].astype(single)
        numer = jnp.einsum('spfa,spoa->sfo', got, blocks)
        denom = jnp.sum(blocks, axis=(1, 3))
        regrid = (numer / denom[:, None, :]).astype(jnp.bfloat16)
        base = (jnp.einsum('sco,ch->sho', states, ocean_weight.astype(single)) + jnp.einsum('sfo,fh->sho', regrid.astype(single), couple_weight.astype(single))).astype(jnp.bfloat16)
        mixed = jnp.einsum('sho,hk->sko', base.astype(single), mix_weight.astype(single))
        result = (base.astype(single) + jax.nn.gelu(mixed)).astype(jnp.bfloat16)
        return jnp.where(water[:, None, None] == 1, result, jnp.zeros_like(result))

    ocean_hidden = lax.map(ocean_device, jnp.arange(LONS, dtype=jnp.int32)).reshape(OTILES, WIDTH, TO)
    return atm_hidden, ocean_hidden
```

```python
import functools

import jax
import jax.numpy as jnp
from jax import lax
from jax.experimental import pallas as pl
from jax.experimental.pallas import tpu as pltpu
from jax.sharding import PartitionSpec as P

TLAT = 16
FOLDB = 2
LANES = 128
MESH = pl.DeviceIdType.MESH
F32 = jnp.float32
BF16 = jnp.bfloat16


def gelu(z):
    return 0.5 * z * (1.0 + jnp.tanh(0.7978845608028654 * (z + 0.044715 * z * z * z)))


def dot(a, b):
    return jnp.dot(a, b, preferred_element_type=F32)


def regroup(blocks, tlat):
    count = len(blocks)
    group = lax.broadcasted_iota(jnp.int32, blocks[0].shape, 1) // tlat
    step = count // 2
    while step:
        low = (group // step) % 2 == 0
        out = list(blocks)
        for i in range(count):
            if (i // step) % 2 == 0:
                first, second = blocks[i], blocks[i + step]
                out[i] = jnp.where(low, first, pltpu.roll(second, step * tlat, 1))
                out[i + step] = jnp.where(low, pltpu.roll(first, LANES - step * tlat, 1), second)
        blocks = out
        step //= 2
    return blocks


def kernel(
    strips,
    pair_ref, mask_ref, atm_hbm, ocean_hbm, lift_ref, conv_hbm, flux_ref, ow_ref, cw_ref, mix_ref, regrid_hbm,
    hid_hbm, oce_hbm,
    xin, conv_v, ocean_v, regrid_v, col, folded_f, wt, lt, ocean_f, wocean, mixt, table, mirror, hid, ustate, oce,
    load_sem, regrid_sem, halo_send, halo_recv, flux_send, flux_recv, mir_sem, hid_sem, oce_sem,
):
    columns, channels, lat = atm_hbm.shape
    width = lift_ref.shape[1]
    och = ow_ref.shape[0]
    fl = flux_ref.shape[0]
    tiles = ocean_hbm.shape[1]
    chunks = lat // LANES
    per = LANES // TLAT
    stride = 3 * channels
    depth = wt.shape[1]

    me = lax.axis_index("lon")
    right = lax.rem(me + 1, strips)
    left = lax.rem(me + strips - 1, strips)
    fold = strips - 1 - me

    def remote(src, dst, send, recv, to):
        return pltpu.make_async_remote_copy(
            src_ref=src, dst_ref=dst, send_sem=send, recv_sem=recv, device_id={"lon": to}, device_id_type=MESH
        )

    barrier = pltpu.get_barrier_semaphore()
    for other in (left, right, fold):
        pl.semaphore_signal(barrier, inc=1, device_id={"lon": other}, device_id_type=MESH)

    load_atm = pltpu.make_async_copy(atm_hbm, xin.at[pl.ds(1, columns)], load_sem.at[0])
    load_conv = pltpu.make_async_copy(conv_hbm, conv_v, load_sem.at[1])
    load_ocean = pltpu.make_async_copy(ocean_hbm, ocean_v, load_sem.at[2])
    load_atm.start()
    load_conv.start()
    load_ocean.start()
    load_main = pltpu.make_async_copy(
        regrid_hbm.at[:, pl.ds(0, 3)], regrid_v.at[:, pl.ds(0, 3)], regrid_sem.at[0]
    )
    load_fold = pltpu.make_async_copy(
        regrid_hbm.at[pl.ds(tiles - FOLDB, FOLDB), pl.ds(3, 1)],
        regrid_v.at[pl.ds(tiles - FOLDB, FOLDB), pl.ds(3, 1)],
        regrid_sem.at[1],
    )
    load_main.start()
    load_fold.start()

    pl.semaphore_wait(barrier, 3)
    halo_r = remote(atm_hbm.at[columns - 1], xin.at[0], halo_send.at[0], halo_recv.at[0], right)
    halo_l = remote(atm_hbm.at[0], xin.at[columns + 1], halo_send.at[1], halo_recv.at[1], left)
    halo_r.start()
    halo_l.start()

    lt[...] = lift_ref[...].astype(F32).T.astype(BF16)
    mixt[...] = mix_ref[...].astype(F32).T.astype(BF16)
    joined = jnp.concatenate(
        [
            ow_ref[...].astype(F32),
            jnp.zeros((96 - och, width), F32),
            cw_ref[...].astype(F32),
            jnp.zeros((LANES - 96 - fl, width), F32),
        ],
        axis=0,
    )
    wocean[...] = joined.T.astype(BF16)

    tail = col.shape[1] - (columns + 1) * stride
    for c in range(chunks):
        col[c, (columns + 1) * stride :, :] = jnp.zeros((tail, LANES), BF16)

    def spread(x):
        v = xin[x].astype(F32)
        lane = lax.broadcasted_iota(jnp.int32, v.shape, 1)
        south = jnp.where(lane == 0, 0.0, pltpu.roll(v, 1, 1))
        north = jnp.where(lane == lat - 1, 0.0, pltpu.roll(v, lat - 1, 1))
        for b, piece in enumerate((south, v, north)):
            piece = piece.astype(BF16)
            rows = pl.ds(pl.multiple_of(x * stride + b * channels, 16), channels)
            for c in range(chunks):
                col[c, rows, :] = piece[:, c * LANES : (c + 1) * LANES]

    load_atm.wait()

    def own(x, carry):
        spread(x + 1)
        return carry

    lax.fori_loop(0, columns, own, 0)

    load_conv.wait()
    for k in range(9):
        folded_f[k * channels : (k + 1) * channels, :] = dot(lift_ref[...], conv_v[k // 3, k % 3])
    folded_f[9 * channels :, :] = jnp.zeros((depth - 9 * channels, width), F32)
    wt[...] = folded_f[...].T.astype(BF16)

    load_ocean.wait()
    ocean_f[...] = ocean_v[...].astype(F32).reshape(ocean_f.shape)
    for t in range(tiles):
        ustate[t, 80:, :] = jnp.zeros((ustate.shape[1] - 80, LANES), BF16)
        ustate[t, 0:och, :] = ocean_f[pl.ds(t, och, stride=tiles), :].astype(BF16)

    halo_r.wait()
    halo_l.wait()
    spread(0)
    spread(columns + 1)

    def flux_copy(c, to, side, index):
        rows = pl.ds(c * per, per)
        return remote(
            table.at[1, rows], table.at[side, rows], flux_send.at[c, index], flux_recv.at[c, index], to
        )

    def hid_copy(c):
        return pltpu.make_async_copy(
            hid.at[c], hid_hbm.at[:, :, pl.ds(pl.multiple_of(c * LANES, LANES), LANES)], hid_sem.at[c]
        )

    to_fold = remote(table.at[1, chunks * per - 1], mirror, mir_sem.at[0], mir_sem.at[1], fold)

    def chunk(i, carry):
        c = chunks - 1 - i
        flux = []
        for x in range(0, columns, 2):
            rhs = jnp.concatenate(
                [col[c, x * stride : x * stride + depth, :], col[c, (x + 1) * stride : (x + 1) * stride + depth, :]],
                axis=1,
            )
            at = (x + 1) * stride + channels
            mid = jnp.concatenate(
                [col[c, at : at + channels, :], col[c, at + stride : at + stride + channels, :]], axis=1
            )
            conv = dot(wt[...], rhs)
            lifted = dot(lt[...], mid).astype(BF16).astype(F32)
            hidden = (lifted + gelu(conv)).astype(BF16)
            hid[c, x] = hidden[:, :LANES]
            hid[c, x + 1] = hidden[:, LANES:]
            f = dot(flux_ref[...], hidden)
            flux += [f[:, :LANES], f[:, LANES:]]
        hid_copy(c).start()
        for a, tile in enumerate(regroup(flux, TLAT)):
            table[1, c * per + a] = tile.astype(BF16)
        flux_copy(c, right, 0, 0).start()
        flux_copy(c, left, 2, 1).start()

        @pl.when(i == 0)
        def _():
            to_fold.start()

        return carry

    lax.fori_loop(0, chunks, chunk, 0)

    load_main.wait()
    load_fold.wait()

    def arrive(c, carry):
        flux_copy(c, right, 0, 0).wait()
        flux_copy(c, left, 2, 1).wait()
        return carry

    lax.fori_loop(0, chunks, arrive, 0)
    to_fold.wait()

    ones = jnp.ones((fl, LANES), BF16)
    mirrored = mirror[...]

    def regrid(t, folded):
        got = [table[p, pair_ref[p, t]] for p in range(3)]
        weights = [regrid_v[t, p] for p in range(3)]
        if folded:
            got.append(mirrored)
            weights.append(regrid_v[t, 3])
        lhs = jnp.concatenate([jnp.concatenate([g, ones], axis=0) for g in got], axis=1)
        rhs = jnp.concatenate(weights, axis=1)
        sums = lax.dot_general(lhs, rhs, (((1,), (1,)), ((), ())), preferred_element_type=F32)
        ustate[t, 96 : 96 + fl, :] = (sums[:fl] / sums[fl : fl + 1]).astype(BF16)

    def encode(t):
        rhs = jnp.concatenate([ustate[t], ustate[t + 1]], axis=1)
        base = dot(wocean[...], rhs).astype(BF16)
        mixed = dot(mixt[...], base)
        result = (base.astype(F32) + gelu(mixed)).astype(BF16)
        for k in range(2):
            water = jnp.full((width, LANES), mask_ref[t + k], jnp.int32) == 1
            oce[t + k] = jnp.where(water, result[:, k * LANES : (k + 1) * LANES].astype(F32), 0.0).astype(BF16)

    def oce_copy(t, index):
        return pltpu.make_async_copy(oce.at[pl.ds(t, 4)], oce_hbm.at[pl.ds(t, 4)], oce_sem.at[index])

    for t in range(tiles):
        regrid(t, t >= tiles - FOLDB)

    for t in range(0, tiles, 2):
        encode(t)
        if t % 4 == 2:
            oce_copy(t - 2, t // 4).start()
    for t in range(0, tiles, 4):
        oce_copy(t, t // 4).wait()

    def leave(c, carry):
        hid_copy(c).wait()
        return carry

    lax.fori_loop(0, chunks, leave, 0)


def per_device(
    strips,
    atm_in,
    ocean_in,
    lift_weight,
    conv_weight,
    flux_weight,
    ocean_weight,
    couple_weight,
    mix_weight,
    regrid_weight,
    pair_tile,
    ocean_mask,
):
    columns, channels, lat = atm_in.shape
    width = lift_weight.shape[1]
    fl = flux_weight.shape[1]
    tiles, och, cells = ocean_in.shape
    chunks = lat // LANES
    stride = 3 * channels
    depth = -(-9 * channels // 256) * 256
    rows = (columns - 1) * stride + depth
    hbm = pl.BlockSpec(memory_space=pl.ANY)
    vmem = pl.BlockSpec(memory_space=pltpu.VMEM)
    smem = pl.BlockSpec(memory_space=pltpu.SMEM)
    dma = pltpu.SemaphoreType.DMA
    flops = 2 * columns * lat * width * (12 * channels) + 2 * tiles * cells * width * (width + 128)
    return pl.pallas_call(
        functools.partial(kernel, strips),
        out_shape=(
            jax.ShapeDtypeStruct((columns, width, lat), BF16),
            jax.ShapeDtypeStruct((tiles, width, cells), BF16),
        ),
        in_specs=[smem, smem, hbm, hbm, vmem, hbm, vmem, vmem, vmem, vmem, hbm],
        out_specs=(hbm, hbm),
        scratch_shapes=[
            pltpu.VMEM((columns + 2, channels, lat), BF16),
            pltpu.VMEM(conv_weight.shape, BF16),
            pltpu.VMEM((och, tiles, cells), BF16),
            pltpu.VMEM(regrid_weight.shape, BF16),
            pltpu.VMEM((chunks, rows, LANES), BF16),
            pltpu.VMEM((depth, width), F32),
            pltpu.VMEM((width, depth), BF16),
            pltpu.VMEM((width, channels), BF16),
            pltpu.VMEM((och * tiles, cells), F32),
            pltpu.VMEM((width, LANES), BF16),
            pltpu.VMEM((width, width), BF16),
            pltpu.VMEM((3, lat // TLAT, fl, LANES), BF16),
            pltpu.VMEM((fl, LANES), BF16),
            pltpu.VMEM((chunks, columns, width, LANES), BF16),
            pltpu.VMEM((tiles, LANES, cells), BF16),
            pltpu.VMEM((tiles, width, cells), BF16),
            dma((3,)),
            dma((2,)),
            dma((2,)),
            dma((2,)),
            dma((chunks, 2)),
            dma((chunks, 2)),
            dma((2,)),
            dma((chunks,)),
            dma((tiles // 4,)),
        ],
        compiler_params=pltpu.CompilerParams(
            collective_id=0, has_side_effects=True, vmem_limit_bytes=56 * 1024 * 1024
        ),
        cost_estimate=pl.CostEstimate(flops=flops, bytes_accessed=8 * 1024 * 1024, transcendentals=2 * 1024 * 1024),
    )(
        pair_tile.T, ocean_mask, atm_in, ocean_in.transpose(1, 0, 2), lift_weight, conv_weight,
        flux_weight.T, ocean_weight, couple_weight, mix_weight, regrid_weight,
    )


def solution(mesh):
    in_specs = (
        P(("groups", "lon"), None, None),
        P(("groups", "lon"), None, None),
        P(),
        P(),
        P(),
        P(),
        P(),
        P(),
        P("lon", None, None, None),
        P("lon", None),
        P("lon"),
    )
    out_specs = (P(("groups", "lon"), None, None), P(("groups", "lon"), None, None))
    return jax.shard_map(
        functools.partial(per_device, mesh.shape["lon"]),
        mesh=mesh,
        in_specs=in_specs,
        out_specs=out_specs,
        check_vma=False,
    )
```

```python
import functools

import jax
import jax.numpy as jnp
from jax import lax
from jax.experimental import pallas as pl
from jax.experimental.pallas import tpu as pltpu
from jax.sharding import PartitionSpec as P

TLAT = 16
FOLDB = 2
MAXACT = 8
LANES = 128
MESH = pl.DeviceIdType.MESH
F32 = jnp.float32
BF16 = jnp.bfloat16


def gelu(z):
    return 0.5 * z * (1.0 + jnp.tanh(0.7978845608028654 * (z + 0.044715 * z * z * z)))


def dot(a, b):
    return jnp.dot(a, b, preferred_element_type=F32)


def regroup(blocks, tlat):
    count = len(blocks)
    group = lax.broadcasted_iota(jnp.int32, blocks[0].shape, 1) // tlat
    step = count // 2
    while step:
        low = (group // step) % 2 == 0
        out = list(blocks)
        for i in range(count):
            if (i // step) % 2 == 0:
                first, second = blocks[i], blocks[i + step]
                out[i] = jnp.where(low, first, pltpu.roll(second, step * tlat, 1))
                out[i + step] = jnp.where(low, pltpu.roll(first, LANES - step * tlat, 1), second)
        blocks = out
        step //= 2
    return blocks


def tally(mask, count):
    ahead = [jnp.int32(0)]
    for t in range(count - 1):
        ahead.append(ahead[-1] + mask[t])
    return ahead


def kernel(
    strips,
    pair_hbm, mask_hbm, atm_hbm, ocean_hbm, lift_hbm, conv_hbm, flux_hbm, regrid_hbm,
    hid_out, packed_out,
    pair_ref, mask_ref, lift_ref, flux_ref, xin, conv_v, ocean_v, regrid_v, col, folded_f, wt, lt, ocean_f, ustate, packed, table, mirror, hid,
    load_sem, regrid_sem, halo_send, halo_recv, flux_send, flux_recv, mir_sem, hid_sem, packed_sem,
):
    columns, channels, lat = atm_hbm.shape
    width = lift_ref.shape[1]
    och, tiles = ocean_hbm.shape[:2]
    fl = flux_ref.shape[0]
    chunks = lat // LANES
    per = LANES // TLAT
    stride = 3 * channels
    depth = wt.shape[1]

    me = lax.axis_index("lon")
    right = lax.rem(me + 1, strips)
    left = lax.rem(me + strips - 1, strips)
    fold = strips - 1 - me

    def remote(src, dst, send, recv, to):
        return pltpu.make_async_remote_copy(
            src_ref=src, dst_ref=dst, send_sem=send, recv_sem=recv, device_id={"lon": to}, device_id_type=MESH
        )

    barrier = pltpu.get_barrier_semaphore()
    for other in (left, right, fold):
        pl.semaphore_signal(barrier, inc=1, device_id={"lon": other}, device_id_type=MESH)

    load_atm = pltpu.make_async_copy(atm_hbm, xin.at[pl.ds(1, columns)], load_sem.at[0])
    load_conv = pltpu.make_async_copy(conv_hbm, conv_v, load_sem.at[1])
    load_ocean = pltpu.make_async_copy(ocean_hbm, ocean_v, load_sem.at[2])
    load_main = pltpu.make_async_copy(
        regrid_hbm.at[:, pl.ds(0, 3)], regrid_v.at[:, pl.ds(0, 3)], regrid_sem.at[0]
    )
    load_fold = pltpu.make_async_copy(
        regrid_hbm.at[pl.ds(tiles - FOLDB, FOLDB), pl.ds(3, 1)],
        regrid_v.at[pl.ds(tiles - FOLDB, FOLDB), pl.ds(3, 1)],
        regrid_sem.at[1],
    )
    smalls = [
        pltpu.make_async_copy(source, target, load_sem.at[3 + i])
        for i, (source, target) in enumerate(
            ((lift_hbm, lift_ref), (flux_hbm, flux_ref), (pair_hbm, pair_ref), (mask_hbm, mask_ref))
        )
    ]
    smalls[0].start()
    load_atm.start()
    load_conv.start()
    for small in smalls[1:]:
        small.start()

    smalls[0].wait()
    lt[...] = lift_ref[...].astype(F32).T.astype(BF16)
    tail = col.shape[1] - (columns + 1) * stride
    for c in range(chunks):
        col[c, (columns + 1) * stride :, :] = jnp.zeros((tail, LANES), BF16)
    folded_f[9 * channels :, :] = jnp.zeros((depth - 9 * channels, width), F32)

    pl.semaphore_wait(barrier, 3)
    halo_r = remote(atm_hbm.at[columns - 1], xin.at[0], halo_send.at[0], halo_recv.at[0], right)
    halo_l = remote(atm_hbm.at[0], xin.at[columns + 1], halo_send.at[1], halo_recv.at[1], left)
    halo_r.start()
    halo_l.start()

    def spread(x):
        v = xin[x].astype(F32)
        lane = lax.broadcasted_iota(jnp.int32, v.shape, 1)
        south = jnp.where(lane == 0, 0.0, pltpu.roll(v, 1, 1))
        north = jnp.where(lane == lat - 1, 0.0, pltpu.roll(v, lat - 1, 1))
        for b, piece in enumerate((south, v, north)):
            piece = piece.astype(BF16)
            at = x * stride + b * channels
            for c in range(chunks):
                col[c, at : at + channels, :] = piece[:, c * LANES : (c + 1) * LANES]

    load_atm.wait()
    load_conv.wait()
    load_ocean.start()
    load_main.start()
    load_fold.start()
    for small in smalls[1:]:
        small.wait()
    for k in range(9):
        folded_f[k * channels : (k + 1) * channels, :] = dot(lift_ref[...], conv_v[k // 3, k % 3])
        if k < columns:
            spread(k + 1)
    wt[...] = folded_f[...].T.astype(BF16)

    halo_r.wait()
    halo_l.wait()
    spread(0)
    spread(columns + 1)

    def flux_copy(c, to, side, index):
        rows = pl.ds(c * per, per)
        return remote(
            table.at[1, rows], table.at[side, rows], flux_send.at[c, index], flux_recv.at[c, index], to
        )

    def hid_copy(c):
        return pltpu.make_async_copy(
            hid.at[c], hid_out.at[:, :, pl.ds(pl.multiple_of(c * LANES, LANES), LANES)], hid_sem.at[c]
        )

    to_fold = remote(table.at[1, chunks * per - 1], mirror, mir_sem.at[0], mir_sem.at[1], fold)

    def chunk(i, carry):
        c = chunks - 1 - i
        flux = []
        for x in range(0, columns, 2):
            rhs = jnp.concatenate(
                [col[c, x * stride : x * stride + depth, :], col[c, (x + 1) * stride : (x + 1) * stride + depth, :]],
                axis=1,
            )
            at = (x + 1) * stride + channels
            mid = jnp.concatenate(
                [col[c, at : at + channels, :], col[c, at + stride : at + stride + channels, :]], axis=1
            )
            conv = dot(wt[...], rhs)
            lifted = dot(lt[...], mid).astype(BF16).astype(F32)
            hidden = (lifted + gelu(conv)).astype(BF16)
            hid[c, x] = hidden[:, :LANES]
            hid[c, x + 1] = hidden[:, LANES:]
            f = dot(flux_ref[...], hidden)
            flux += [f[:, :LANES], f[:, LANES:]]
        hid_copy(c).start()
        for a, tile in enumerate(regroup(flux, TLAT)):
            table[1, c * per + a] = tile.astype(BF16)
        flux_copy(c, right, 0, 0).start()
        flux_copy(c, left, 2, 1).start()

        @pl.when(i == 0)
        def _():
            to_fold.start()

        return carry

    lax.fori_loop(0, chunks, chunk, 0)

    load_ocean.wait()
    ocean_f[...] = ocean_v[...].astype(F32).reshape(ocean_f.shape)
    for t in range(tiles):
        ustate[t, 80:, :] = jnp.zeros((ustate.shape[1] - 80, LANES), BF16)
        ustate[t, 0:och, :] = ocean_f[pl.ds(t, och, stride=tiles), :].astype(BF16)

    plain = tiles - FOLDB
    ahead = tally(mask_ref, plain)
    slots = []
    for k in range(MAXACT - FOLDB):
        slot = jnp.int32(0)
        for t in range(k, plain):
            slot = jnp.where((mask_ref[t] == 1) & (ahead[t] == k), t, slot)
        slots.append(slot)
    slots += [plain + k for k in range(FOLDB)]
    for k, t in enumerate(slots):
        packed[k // 2, :, (k % 2) * LANES : (k % 2 + 1) * LANES] = ustate[t]

    load_main.wait()
    load_fold.wait()

    def arrive(c, carry):
        flux_copy(c, right, 0, 0).wait()
        flux_copy(c, left, 2, 1).wait()
        return carry

    lax.fori_loop(0, chunks, arrive, 0)
    to_fold.wait()

    ones = jnp.ones((fl, LANES), BF16)
    mirrored = mirror[...]
    for k, t in enumerate(slots):
        got = [table[p, pair_ref[p, t]] for p in range(3)]
        weights = [regrid_v[t, p] for p in range(3)]
        if k >= MAXACT - FOLDB:
            got.append(mirrored)
            weights.append(regrid_v[t, 3])
        lhs = jnp.concatenate([jnp.concatenate([g, ones], axis=0) for g in got], axis=1)
        rhs = jnp.concatenate(weights, axis=1)
        sums = lax.dot_general(lhs, rhs, (((1,), (1,)), ((), ())), preferred_element_type=F32)
        packed[k // 2, 96 : 96 + fl, (k % 2) * LANES : (k % 2 + 1) * LANES] = (
            sums[:fl] / sums[fl : fl + 1]
        ).astype(BF16)

    out = pltpu.make_async_copy(packed, packed_out, packed_sem)
    out.start()

    def leave(c, carry):
        hid_copy(c).wait()
        return carry

    lax.fori_loop(0, chunks, leave, 0)
    out.wait()


def finish(
    mask_ref, hid_in, packed_in, ow_ref, cw_ref, mix_ref,
    hid_hbm, oce_hbm,
    packed, wocean, mixt, oce, packed_sem, hid_sem, oce_sem,
):
    tiles = oce_hbm.shape[0]
    och, width = ow_ref.shape
    fl = cw_ref.shape[0]
    get = pltpu.make_async_copy(packed_in, packed, packed_sem)
    get.start()
    keep = pltpu.make_async_copy(hid_in, hid_hbm, hid_sem)
    keep.start()

    mixt[...] = mix_ref[...].astype(F32).T.astype(BF16)
    joined = jnp.concatenate(
        [
            ow_ref[...].astype(F32),
            jnp.zeros((96 - och, width), F32),
            cw_ref[...].astype(F32),
            jnp.zeros((LANES - 96 - fl, width), F32),
        ],
        axis=0,
    )
    wocean[...] = joined.T.astype(BF16)
    oce[MAXACT] = jnp.zeros((width, LANES), BF16)
    get.wait()
    for k in range(0, MAXACT, 2):
        base = dot(wocean[...], packed[k // 2]).astype(BF16)
        mixed = dot(mixt[...], base)
        result = (base.astype(F32) + gelu(mixed)).astype(BF16)
        oce[k] = result[:, :LANES]
        oce[k + 1] = result[:, LANES:]

    plain = tiles - FOLDB
    ahead = tally(mask_ref, plain)
    copies = []
    for t in range(tiles):
        slot = ahead[t] if t < plain else jnp.int32(MAXACT - FOLDB + t - plain)
        slot = jnp.where(mask_ref[t] == 1, slot, MAXACT)
        copies.append(pltpu.make_async_copy(oce.at[slot], oce_hbm.at[t], oce_sem.at[t]))
        copies[-1].start()
    for copy in copies:
        copy.wait()
    keep.wait()


def per_device(
    strips,
    atm_in,
    ocean_in,
    lift_weight,
    conv_weight,
    flux_weight,
    ocean_weight,
    couple_weight,
    mix_weight,
    regrid_weight,
    pair_tile,
    ocean_mask,
):
    columns, channels, lat = atm_in.shape
    width = lift_weight.shape[1]
    fl = flux_weight.shape[1]
    tiles, och, cells = ocean_in.shape
    chunks = lat // LANES
    stride = 3 * channels
    depth = -(-9 * channels // 256) * 256
    rows = (columns - 1) * stride + depth
    hbm = pl.BlockSpec(memory_space=pltpu.HBM)
    anywhere = pl.BlockSpec(memory_space=pl.ANY)
    vmem = pl.BlockSpec(memory_space=pltpu.VMEM)
    smem = pl.BlockSpec(memory_space=pltpu.SMEM)
    dma = pltpu.SemaphoreType.DMA
    hidden, packed = pl.pallas_call(
        functools.partial(kernel, strips),
        out_shape=(
            pltpu.VMEM((columns, width, lat), BF16),
            pltpu.VMEM((MAXACT // 2, LANES, 2 * cells), BF16),
        ),
        in_specs=[hbm] * 8,
        out_specs=(anywhere, anywhere),
        scratch_shapes=[
            pltpu.SMEM(pair_tile.shape[::-1], jnp.int32),
            pltpu.SMEM(ocean_mask.shape, jnp.int32),
            pltpu.VMEM(lift_weight.shape, BF16),
            pltpu.VMEM(flux_weight.shape[::-1], BF16),
            pltpu.VMEM((columns + 2, channels, lat), BF16),
            pltpu.VMEM(conv_weight.shape, BF16),
            pltpu.VMEM((och, tiles, cells), BF16),
            pltpu.VMEM(regrid_weight.shape, BF16),
            pltpu.VMEM((chunks, rows, LANES), BF16),
            pltpu.VMEM((depth, width), F32),
            pltpu.VMEM((width, depth), BF16),
            pltpu.VMEM((width, channels), BF16),
            pltpu.VMEM((och * tiles, cells), F32),
            pltpu.VMEM((tiles, LANES, cells), BF16),
            pltpu.VMEM((MAXACT // 2, LANES, 2 * cells), BF16),
            pltpu.VMEM((3, lat // TLAT, fl, LANES), BF16),
            pltpu.VMEM((fl, LANES), BF16),
            pltpu.VMEM((chunks, columns, width, LANES), BF16),
            dma((7,)),
            dma((2,)),
            dma((2,)),
            dma((2,)),
            dma((chunks, 2)),
            dma((chunks, 2)),
            dma((2,)),
            dma((chunks,)),
            dma,
        ],
        compiler_params=pltpu.CompilerParams(
            collective_id=0, has_side_effects=True, vmem_limit_bytes=61 * 1024 * 1024
        ),
        cost_estimate=pl.CostEstimate(
            flops=24 * columns * lat * width * channels, bytes_accessed=8 * 1024 * 1024, transcendentals=1024 * 1024
        ),
    )(
        pair_tile.T, ocean_mask, atm_in, ocean_in.transpose(1, 0, 2), lift_weight, conv_weight,
        flux_weight.T, regrid_weight,
    )
    return pl.pallas_call(
        finish,
        out_shape=(
            jax.ShapeDtypeStruct((columns, width, lat), BF16),
            jax.ShapeDtypeStruct((tiles, width, cells), BF16),
        ),
        in_specs=[smem, anywhere, anywhere, vmem, vmem, vmem],
        out_specs=(anywhere, anywhere),
        scratch_shapes=[
            pltpu.VMEM((MAXACT // 2, LANES, 2 * cells), BF16),
            pltpu.VMEM((width, LANES), BF16),
            pltpu.VMEM((width, width), BF16),
            pltpu.VMEM((MAXACT + 1, width, cells), BF16),
            dma,
            dma,
            dma((tiles,)),
        ],
        compiler_params=pltpu.CompilerParams(vmem_limit_bytes=50 * 1024 * 1024),
        cost_estimate=pl.CostEstimate(
            flops=2 * MAXACT * cells * width * (width + 128), bytes_accessed=8 * 1024 * 1024, transcendentals=1024 * 1024
        ),
    )(ocean_mask, hidden, packed, ocean_weight, couple_weight, mix_weight)


def solution(mesh):
    in_specs = (
        P(("groups", "lon"), None, None),
        P(("groups", "lon"), None, None),
        P(),
        P(),
        P(),
        P(),
        P(),
        P(),
        P("lon", None, None, None),
        P("lon", None),
        P("lon"),
    )
    out_specs = (P(("groups", "lon"), None, None), P(("groups", "lon"), None, None))
    return jax.shard_map(
        functools.partial(per_device, mesh.shape["lon"]),
        mesh=mesh,
        in_specs=in_specs,
        out_specs=out_specs,
        check_vma=False,
    )
```

```python
import functools

import jax
import jax.numpy as jnp
from jax import lax
from jax.experimental import pallas as pl
from jax.experimental.pallas import tpu as pltpu
from jax.sharding import PartitionSpec as P

TLAT = 16
FOLDB = 2
MAXACT = 8
LANES = 128
MESH = pl.DeviceIdType.MESH
F32 = jnp.float32
BF16 = jnp.bfloat16


def half_gelu(h):
    return h * jnp.tanh(h * (1.5957691216057308 + 0.285419265090401 * (h * h)))


def dot(a, b):
    return jnp.dot(a, b, preferred_element_type=F32)


def regroup(blocks, tlat):
    count = len(blocks)
    group = lax.broadcasted_iota(jnp.int32, blocks[0].shape, 1) // tlat
    step = count // 2
    while step:
        low = (group // step) % 2 == 0
        out = list(blocks)
        for i in range(count):
            if (i // step) % 2 == 0:
                first, second = blocks[i], blocks[i + step]
                out[i] = jnp.where(low, first, pltpu.roll(second, step * tlat, 1))
                out[i + step] = jnp.where(low, pltpu.roll(first, LANES - step * tlat, 1), second)
        blocks = out
        step //= 2
    return blocks


def water_slots(mask, tiles):
    plain = tiles - FOLDB
    slots = [jnp.int32(0)] * (MAXACT - FOLDB)
    count = jnp.int32(0)
    for t in range(plain):
        wet = mask[t] == 1
        for k in range(min(t + 1, MAXACT - FOLDB)):
            slots[k] = jnp.where(wet & (count == k), t, slots[k])
        count = count + mask[t]
    return slots + [plain + k for k in range(FOLDB)], count


def kernel(
    strips,
    pair_hbm, mask_hbm, atm_hbm, ocean_hbm, lift_hbm, conv_hbm, flux_hbm, regrid_hbm,
    hid_out, packed_out,
    pair_ref, mask_ref, lift_ref, flux_ref, xin, conv_v, ocean_v, regrid_v, col, folded_f, wt, lt, ocean_f, ustate, table, mirror,
    load_sem, regrid_sem, halo_send, halo_recv, flux_send, flux_recv, mir_sem,
):
    columns, channels, lat = atm_hbm.shape
    width = lift_ref.shape[1]
    och, tiles = ocean_hbm.shape[:2]
    fl = flux_ref.shape[0]
    chunks = lat // LANES
    per = LANES // TLAT
    stride = 3 * channels
    depth = wt.shape[1]

    me = lax.axis_index("lon")
    right = lax.rem(me + 1, strips)
    left = lax.rem(me + strips - 1, strips)
    fold = strips - 1 - me

    def remote(src, dst, send, recv, to):
        return pltpu.make_async_remote_copy(
            src_ref=src, dst_ref=dst, send_sem=send, recv_sem=recv, device_id={"lon": to}, device_id_type=MESH
        )

    barrier = pltpu.get_barrier_semaphore()
    for other in (left, right, fold):
        pl.semaphore_signal(barrier, inc=1, device_id={"lon": other}, device_id_type=MESH)

    load_atm = pltpu.make_async_copy(atm_hbm, xin.at[pl.ds(1, columns)], load_sem.at[0])
    load_conv = pltpu.make_async_copy(conv_hbm, conv_v, load_sem.at[1])
    load_ocean = pltpu.make_async_copy(ocean_hbm, ocean_v, load_sem.at[2])
    load_main = pltpu.make_async_copy(
        regrid_hbm.at[:, pl.ds(0, 3)], regrid_v.at[:, pl.ds(0, 3)], regrid_sem.at[0]
    )
    load_fold = pltpu.make_async_copy(
        regrid_hbm.at[pl.ds(tiles - FOLDB, FOLDB), pl.ds(3, 1)],
        regrid_v.at[pl.ds(tiles - FOLDB, FOLDB), pl.ds(3, 1)],
        regrid_sem.at[1],
    )
    smalls = [
        pltpu.make_async_copy(source, target, load_sem.at[3 + i])
        for i, (source, target) in enumerate(
            ((lift_hbm, lift_ref), (flux_hbm, flux_ref), (pair_hbm, pair_ref), (mask_hbm, mask_ref))
        )
    ]
    smalls[0].start()
    load_atm.start()
    load_conv.start()
    for small in smalls[1:]:
        small.start()

    smalls[0].wait()
    lt[...] = lift_ref[...].astype(F32).T.astype(BF16)
    tail = col.shape[1] - (columns + 1) * stride
    for c in range(chunks):
        col[c, (columns + 1) * stride :, :] = jnp.zeros((tail, LANES), BF16)
    folded_f[9 * channels :, :] = jnp.zeros((depth - 9 * channels, width), F32)

    pl.semaphore_wait(barrier, 3)
    halo_r = remote(atm_hbm.at[columns - 1], xin.at[0], halo_send.at[0], halo_recv.at[0], right)
    halo_l = remote(atm_hbm.at[0], xin.at[columns + 1], halo_send.at[1], halo_recv.at[1], left)
    halo_r.start()
    halo_l.start()

    def spread(x):
        v = xin[x].astype(F32)
        lane = lax.broadcasted_iota(jnp.int32, v.shape, 1)
        south = jnp.where(lane == 0, 0.0, pltpu.roll(v, 1, 1))
        north = jnp.where(lane == lat - 1, 0.0, pltpu.roll(v, lat - 1, 1))
        for b, piece in enumerate((south, v, north)):
            piece = piece.astype(BF16)
            at = x * stride + b * channels
            for c in range(chunks):
                col[c, at : at + channels, :] = piece[:, c * LANES : (c + 1) * LANES]

    load_atm.wait()
    load_conv.wait()
    load_ocean.start()
    load_main.start()
    load_fold.start()
    for small in smalls[1:]:
        small.wait()
    for k in range(9):
        folded_f[k * channels : (k + 1) * channels, :] = dot(lift_ref[...], conv_v[k // 3, k % 3])
        if k < columns:
            spread(k + 1)
    wt[...] = (0.5 * folded_f[...]).T.astype(BF16)

    halo_r.wait()
    halo_l.wait()
    spread(0)
    spread(columns + 1)

    def flux_copy(c, to, side, index):
        rows = pl.ds(c * per, per)
        return remote(
            table.at[1, rows], table.at[side, rows], flux_send.at[c, index], flux_recv.at[c, index], to
        )

    to_fold = remote(table.at[1, chunks * per - 1], mirror, mir_sem.at[0], mir_sem.at[1], fold)

    def convolve(c, x):
        rhs = jnp.concatenate(
            [col[c, x * stride : x * stride + depth, :], col[c, (x + 1) * stride : (x + 1) * stride + depth, :]],
            axis=1,
        )
        at = (x + 1) * stride + channels
        mid = jnp.concatenate([col[c, at : at + channels, :], col[c, at + stride : at + stride + channels, :]], axis=1)
        return dot(wt[...], rhs), dot(lt[...], mid)

    def activate(c, x, half, lifted):
        hidden = (lifted + half + half_gelu(half)).astype(BF16)
        hid_out[x, :, c * LANES : (c + 1) * LANES] = hidden[:, :LANES]
        hid_out[x + 1, :, c * LANES : (c + 1) * LANES] = hidden[:, LANES:]
        f = dot(flux_ref[...], hidden)
        return [f[:, :LANES], f[:, LANES:]]

    def send(c, flux):
        for a, tile in enumerate(regroup(flux, TLAT)):
            table[1, c * per + a] = tile.astype(BF16)
        flux_copy(c, right, 0, 0).start()
        flux_copy(c, left, 2, 1).start()
        if c == chunks - 1:
            to_fold.start()

    work = [(c, x) for c in reversed(range(chunks)) for x in range(0, columns, 2)]
    flux = []
    ready = convolve(*work[0])
    for i, (c, x) in enumerate(work):
        now = ready
        if i + 1 < len(work):
            ready = convolve(*work[i + 1])
        flux += activate(c, x, *now)
        if len(flux) == columns:
            send(c, flux)
            flux = []

    load_ocean.wait()
    ocean_f[...] = ocean_v[...].astype(F32).reshape(ocean_f.shape)
    for t in range(tiles):
        ustate[t, 80:, :] = jnp.zeros((ustate.shape[1] - 80, LANES), BF16)
        ustate[t, 0:och, :] = ocean_f[pl.ds(t, och, stride=tiles), :].astype(BF16)

    slots, _ = water_slots(mask_ref, tiles)
    for k, t in enumerate(slots):
        packed_out[k // 2, :, (k % 2) * LANES : (k % 2 + 1) * LANES] = ustate[t]

    load_main.wait()
    load_fold.wait()

    def arrive(c, carry):
        flux_copy(c, right, 0, 0).wait()
        flux_copy(c, left, 2, 1).wait()
        return carry

    lax.fori_loop(0, chunks, arrive, 0)
    to_fold.wait()

    ones = jnp.ones((fl, LANES), BF16)
    mirrored = mirror[...]
    for k, t in enumerate(slots):
        got = [table[p, pair_ref[p, t]] for p in range(3)]
        weights = [regrid_v[t, p] for p in range(3)]
        if k >= MAXACT - FOLDB:
            got.append(mirrored)
            weights.append(regrid_v[t, 3])
        lhs = jnp.concatenate([jnp.concatenate([g, ones], axis=0) for g in got], axis=1)
        rhs = jnp.concatenate(weights, axis=1)
        sums = lax.dot_general(lhs, rhs, (((1,), (1,)), ((), ())), preferred_element_type=F32)
        packed_out[k // 2, 96 : 96 + fl, (k % 2) * LANES : (k % 2 + 1) * LANES] = (
            sums[:fl] / sums[fl : fl + 1]
        ).astype(BF16)


def finish(
    mask_ref, hid_in, packed, ow_ref, cw_ref, mix_ref,
    hid_hbm, oce_hbm,
    wocean, mixt, oce, hid_sem, land_sem, water_sem,
):
    tiles = oce_hbm.shape[0]
    och, width = ow_ref.shape
    fl = cw_ref.shape[0]
    keep = pltpu.make_async_copy(hid_in, hid_hbm, hid_sem)
    keep.start()

    plain = tiles - FOLDB
    oce[MAXACT] = jnp.zeros((width, LANES), BF16)
    land = [pltpu.make_async_copy(oce.at[MAXACT], oce_hbm.at[t], land_sem.at[t]) for t in range(plain)]
    for t in range(plain):
        pl.when(mask_ref[t] == 0)(land[t].start)

    slots, count = water_slots(mask_ref, tiles)
    water = [pltpu.make_async_copy(oce.at[k], oce_hbm.at[t], water_sem.at[k]) for k, t in enumerate(slots)]

    def if_water(k, act):
        if k < MAXACT - FOLDB:
            pl.when(k < count)(act)
        else:
            act()

    mixt[...] = mix_ref[...].astype(F32).T.astype(BF16)
    joined = jnp.concatenate(
        [
            ow_ref[...].astype(F32),
            jnp.zeros((96 - och, width), F32),
            cw_ref[...].astype(F32),
            jnp.zeros((LANES - 96 - fl, width), F32),
        ],
        axis=0,
    )
    wocean[...] = joined.T.astype(BF16)
    for first in range(0, MAXACT, 4):
        for k in range(first, first + 4, 2):
            base = dot(wocean[...], packed[k // 2]).astype(BF16)
            half = 0.5 * dot(mixt[...], base)
            result = (base.astype(F32) + half + half_gelu(half)).astype(BF16)
            oce[k] = result[:, :LANES]
            oce[k + 1] = result[:, LANES:]
        for k in range(first, first + 4):
            if_water(k, water[k].start)

    for k in range(MAXACT):
        if_water(k, water[k].wait)
    for t in range(plain):
        pl.when(mask_ref[t] == 0)(land[t].wait)
    keep.wait()


def per_device(
    strips,
    atm_in,
    ocean_in,
    lift_weight,
    conv_weight,
    flux_weight,
    ocean_weight,
    couple_weight,
    mix_weight,
    regrid_weight,
    pair_tile,
    ocean_mask,
):
    columns, channels, lat = atm_in.shape
    width = lift_weight.shape[1]
    fl = flux_weight.shape[1]
    tiles, och, cells = ocean_in.shape
    chunks = lat // LANES
    stride = 3 * channels
    depth = -(-9 * channels // 256) * 256
    rows = (columns - 1) * stride + depth
    hbm = pl.BlockSpec(memory_space=pltpu.HBM)
    anywhere = pl.BlockSpec(memory_space=pl.ANY)
    vmem = pl.BlockSpec(memory_space=pltpu.VMEM)
    smem = pl.BlockSpec(memory_space=pltpu.SMEM)
    dma = pltpu.SemaphoreType.DMA
    hidden, packed = pl.pallas_call(
        functools.partial(kernel, strips),
        out_shape=(
            pltpu.VMEM((columns, width, lat), BF16),
            pltpu.VMEM((MAXACT // 2, LANES, 2 * cells), BF16),
        ),
        in_specs=[hbm] * 8,
        out_specs=(vmem, vmem),
        scratch_shapes=[
            pltpu.SMEM(pair_tile.shape[::-1], jnp.int32),
            pltpu.SMEM(ocean_mask.shape, jnp.int32),
            pltpu.VMEM(lift_weight.shape, BF16),
            pltpu.VMEM(flux_weight.shape[::-1], BF16),
            pltpu.VMEM((columns + 2, channels, lat), BF16),
            pltpu.VMEM(conv_weight.shape, BF16),
            pltpu.VMEM((och, tiles, cells), BF16),
            pltpu.VMEM(regrid_weight.shape, BF16),
            pltpu.VMEM((chunks, rows, LANES), BF16),
            pltpu.VMEM((depth, width), F32),
            pltpu.VMEM((width, depth), BF16),
            pltpu.VMEM((width, channels), BF16),
            pltpu.VMEM((och * tiles, cells), F32),
            pltpu.VMEM((tiles, LANES, cells), BF16),
            pltpu.VMEM((3, lat // TLAT, fl, LANES), BF16),
            pltpu.VMEM((fl, LANES), BF16),
            dma((7,)),
            dma((2,)),
            dma((2,)),
            dma((2,)),
            dma((chunks, 2)),
            dma((chunks, 2)),
            dma((2,)),
        ],
        compiler_params=pltpu.CompilerParams(
            collective_id=0, has_side_effects=True, vmem_limit_bytes=61 * 1024 * 1024
        ),
        cost_estimate=pl.CostEstimate(
            flops=24 * columns * lat * width * channels, bytes_accessed=8 * 1024 * 1024, transcendentals=1024 * 1024
        ),
    )(
        pair_tile.T, ocean_mask, atm_in, ocean_in.transpose(1, 0, 2), lift_weight, conv_weight,
        flux_weight.T, regrid_weight,
    )
    return pl.pallas_call(
        finish,
        out_shape=(
            jax.ShapeDtypeStruct((columns, width, lat), BF16),
            jax.ShapeDtypeStruct((tiles, width, cells), BF16),
        ),
        in_specs=[smem, anywhere, vmem, vmem, vmem, vmem],
        out_specs=(anywhere, anywhere),
        scratch_shapes=[
            pltpu.VMEM((width, LANES), BF16),
            pltpu.VMEM((width, width), BF16),
            pltpu.VMEM((MAXACT + 1, width, cells), BF16),
            dma,
            dma((tiles,)),
            dma((MAXACT,)),
        ],
        compiler_params=pltpu.CompilerParams(vmem_limit_bytes=50 * 1024 * 1024),
        cost_estimate=pl.CostEstimate(
            flops=2 * MAXACT * cells * width * (width + 128), bytes_accessed=8 * 1024 * 1024, transcendentals=1024 * 1024
        ),
    )(ocean_mask, hidden, packed, ocean_weight, couple_weight, mix_weight)


def solution(mesh):
    in_specs = (
        P(("groups", "lon"), None, None),
        P(("groups", "lon"), None, None),
        P(),
        P(),
        P(),
        P(),
        P(),
        P(),
        P("lon", None, None, None),
        P("lon", None),
        P("lon"),
    )
    out_specs = (P(("groups", "lon"), None, None), P(("groups", "lon"), None, None))
    return jax.shard_map(
        functools.partial(per_device, mesh.shape["lon"]),
        mesh=mesh,
        in_specs=in_specs,
        out_specs=out_specs,
        check_vma=False,
    )
```

```python
import functools

import jax
import jax.numpy as jnp
from jax import lax
from jax.experimental import pallas as pl
from jax.experimental.pallas import tpu as pltpu
from jax.sharding import PartitionSpec as P

TLAT = 16
FOLDB = 2
MAXACT = 8
LANES = 128
MESH = pl.DeviceIdType.MESH
F32 = jnp.float32
BF16 = jnp.bfloat16


def half_gelu(h):
    return h * jnp.tanh(h * (1.5957691216057308 + 0.285419265090401 * (h * h)))


def dot(a, b):
    return jnp.dot(a, b, preferred_element_type=F32)


def regroup(blocks, tlat):
    count = len(blocks)
    group = lax.broadcasted_iota(jnp.int32, blocks[0].shape, 1) // tlat
    step = count // 2
    while step:
        low = (group // step) % 2 == 0
        out = list(blocks)
        for i in range(count):
            if (i // step) % 2 == 0:
                first, second = blocks[i], blocks[i + step]
                out[i] = jnp.where(low, first, pltpu.roll(second, step * tlat, 1))
                out[i + step] = jnp.where(low, pltpu.roll(first, LANES - step * tlat, 1), second)
        blocks = out
        step //= 2
    return blocks


def water_slots(mask, tiles):
    plain = tiles - FOLDB
    slots = [jnp.int32(0)] * (MAXACT - FOLDB)
    count = jnp.int32(0)
    for t in range(plain):
        wet = mask[t] == 1
        for k in range(min(t + 1, MAXACT - FOLDB)):
            slots[k] = jnp.where(wet & (count == k), t, slots[k])
        count = count + mask[t]
    return slots + [plain + k for k in range(FOLDB)]


def kernel(
    strips,
    pair_hbm, mask_hbm, atm_hbm, ocean_hbm, lift_hbm, conv_hbm, flux_hbm, ow_hbm, cw_hbm, mix_hbm, regrid_hbm,
    hid_out, packed_out, wocean_out, mixt_out, from_hbm,
    pair_ref, mask_ref, from_ref, lift_ref, flux_ref, ow_ref, cw_ref, mix_ref, xin, conv_v, ocean_v, regrid_v, col, folded_f, wt, lt, ocean_f, ustate, mine, sides, mirror, partial,
    load_sem, regrid_sem, halo_send, halo_recv, flux_send, flux_recv, mir_sem,
):
    columns, channels, lat = atm_hbm.shape
    width = lift_ref.shape[1]
    och, tiles = ocean_hbm.shape[:2]
    fl = flux_ref.shape[0]
    chunks = lat // LANES
    per = LANES // TLAT
    stride = 3 * channels
    depth = wt.shape[1]

    me = lax.axis_index("lon")
    right = lax.rem(me + 1, strips)
    left = lax.rem(me + strips - 1, strips)
    fold = strips - 1 - me

    def remote(src, dst, send, recv, to):
        return pltpu.make_async_remote_copy(
            src_ref=src, dst_ref=dst, send_sem=send, recv_sem=recv, device_id={"lon": to}, device_id_type=MESH
        )

    barrier = pltpu.get_barrier_semaphore()
    for other in (left, right, fold):
        pl.semaphore_signal(barrier, inc=1, device_id={"lon": other}, device_id_type=MESH)

    load_atm = pltpu.make_async_copy(atm_hbm, xin.at[pl.ds(1, columns)], load_sem.at[0])
    load_conv = pltpu.make_async_copy(conv_hbm, conv_v, load_sem.at[1])
    load_ocean = pltpu.make_async_copy(ocean_hbm, ocean_v, load_sem.at[2])
    load_main = pltpu.make_async_copy(
        regrid_hbm.at[:, pl.ds(0, 3)], regrid_v.at[:, pl.ds(0, 3)], regrid_sem.at[0]
    )
    load_fold = pltpu.make_async_copy(
        regrid_hbm.at[pl.ds(tiles - FOLDB, FOLDB), pl.ds(3, 1)],
        regrid_v.at[pl.ds(tiles - FOLDB, FOLDB), pl.ds(3, 1)],
        regrid_sem.at[1],
    )
    load_ows = [
        pltpu.make_async_copy(source, target, load_sem.at[7 + i])
        for i, (source, target) in enumerate(((ow_hbm, ow_ref), (cw_hbm, cw_ref), (mix_hbm, mix_ref)))
    ]
    smalls = [
        pltpu.make_async_copy(source, target, load_sem.at[3 + i])
        for i, (source, target) in enumerate(
            ((lift_hbm, lift_ref), (flux_hbm, flux_ref), (pair_hbm, pair_ref), (mask_hbm, mask_ref))
        )
    ]
    smalls[0].start()
    load_atm.start()
    load_conv.start()
    for small in smalls[1:]:
        small.start()

    smalls[0].wait()
    lt[...] = lift_ref[...].astype(F32).T.astype(BF16)
    tail = col.shape[1] - (columns + 1) * stride
    for c in range(chunks):
        col[c, (columns + 1) * stride :, :] = jnp.zeros((tail, LANES), BF16)
    folded_f[9 * channels :, :] = jnp.zeros((depth - 9 * channels, width), F32)

    pl.semaphore_wait(barrier, 3)
    halo_r = remote(atm_hbm.at[columns - 1], xin.at[0], halo_send.at[0], halo_recv.at[0], right)
    halo_l = remote(atm_hbm.at[0], xin.at[columns + 1], halo_send.at[1], halo_recv.at[1], left)
    halo_r.start()
    halo_l.start()

    def spread(x):
        v = xin[x].astype(F32)
        lane = lax.broadcasted_iota(jnp.int32, v.shape, 1)
        south = jnp.where(lane == 0, 0.0, pltpu.roll(v, 1, 1))
        north = jnp.where(lane == lat - 1, 0.0, pltpu.roll(v, lat - 1, 1))
        for b, piece in enumerate((south, v, north)):
            piece = piece.astype(BF16)
            at = x * stride + b * channels
            for c in range(chunks):
                col[c, at : at + channels, :] = piece[:, c * LANES : (c + 1) * LANES]

    load_atm.wait()
    load_conv.wait()
    load_ocean.start()
    for load in load_ows:
        load.start()
    load_main.start()
    load_fold.start()
    for small in smalls[1:]:
        small.wait()
    for k in range(9):
        folded_f[k * channels : (k + 1) * channels, :] = dot(lift_ref[...], conv_v[k // 3, k % 3])
        if k < columns:
            spread(k + 1)
    wt[...] = (0.5 * folded_f[...]).T.astype(BF16)

    def flux_copy(c, to, side):
        rows = pl.ds(c * per, per)
        return remote(
            mine.at[rows], sides.at[side, rows], flux_send.at[c, side], flux_recv.at[c, side], to
        )

    to_fold = remote(mine.at[chunks * per - 1], mirror, mir_sem.at[0], mir_sem.at[1], fold)

    def convolve(c, x):
        rhs = jnp.concatenate(
            [col[c, x * stride : x * stride + depth, :], col[c, (x + 1) * stride : (x + 1) * stride + depth, :]],
            axis=1,
        )
        at = (x + 1) * stride + channels
        mid = jnp.concatenate([col[c, at : at + channels, :], col[c, at + stride : at + stride + channels, :]], axis=1)
        return dot(wt[...], rhs), dot(lt[...], mid)

    def activate(c, x, half, lifted):
        hidden = (lifted + half + half_gelu(half)).astype(BF16)
        hid_out[x, :, c * LANES : (c + 1) * LANES] = hidden[:, :LANES]
        hid_out[x + 1, :, c * LANES : (c + 1) * LANES] = hidden[:, LANES:]
        f = dot(flux_ref[...], hidden)
        return [f[:, :LANES], f[:, LANES:]]

    def send(c, flux):
        for a, tile in enumerate(regroup(flux, TLAT)):
            mine[c * per + a] = tile.astype(BF16)
        flux_copy(c, right, 0).start()
        flux_copy(c, left, 1).start()
        if c == chunks - 1:
            to_fold.start()

    def sweep(work):
        ready = convolve(*work[0])
        for i, (c, x) in enumerate(work):
            now = ready
            if i + 1 < len(work):
                ready = convolve(*work[i + 1])
            flux[c, x], flux[c, x + 1] = activate(c, x, *now)
            if x + 2 == columns:
                send(c, [flux.pop((c, k)) for k in range(columns)])

    flux = {}
    bands = list(reversed(range(chunks)))
    sweep([(c, x) for c in bands for x in range(2, columns - 2, 2)])
    halo_r.wait()
    halo_l.wait()
    spread(0)
    spread(columns + 1)

    sweep([(c, x) for c in bands for x in (0, columns - 2)])

    load_ocean.wait()
    ocean_f[...] = ocean_v[...].astype(F32).reshape(ocean_f.shape)
    for t in range(tiles):
        ustate[t, 80:, :] = jnp.zeros((ustate.shape[1] - 80, LANES), BF16)
        ustate[t, 0:och, :] = ocean_f[pl.ds(t, och, stride=tiles), :].astype(BF16)

    slots = water_slots(mask_ref, tiles)
    ahead = jnp.int32(0)
    for t in range(tiles):
        slot = ahead if t < tiles - FOLDB else jnp.int32(MAXACT - tiles + t)
        from_ref[t] = jnp.where(mask_ref[t] == 1, slot, MAXACT)
        ahead = ahead + mask_ref[t]
    give_from = pltpu.make_async_copy(from_ref, from_hbm, load_sem.at[10])
    give_from.start()
    for k, t in enumerate(slots):
        packed_out[k // 2, :, (k % 2) * LANES : (k % 2 + 1) * LANES] = ustate[t]

    for load in load_ows:
        load.wait()
    mixt_out[...] = (0.5 * mix_ref[...].astype(F32)).T.astype(BF16)
    joined = jnp.concatenate(
        [
            ow_ref[...].astype(F32),
            jnp.zeros((96 - och, width), F32),
            cw_ref[...].astype(F32),
            jnp.zeros((LANES - 96 - fl, width), F32),
        ],
        axis=0,
    )
    wocean_out[...] = joined.T.astype(BF16)

    load_main.wait()
    load_fold.wait()
    ones = jnp.ones((fl, LANES), BF16)

    def weigh(t, blocks, got):
        lhs = jnp.concatenate([jnp.concatenate([g, ones], axis=0) for g in got], axis=1)
        rhs = jnp.concatenate([regrid_v[t, p] for p in blocks], axis=1)
        return lax.dot_general(lhs, rhs, (((1,), (1,)), ((), ())), preferred_element_type=F32)

    for k, t in enumerate(slots):
        partial[k] = weigh(t, (1,), [mine[pair_ref[1, t]]])

    def arrive(c, carry):
        flux_copy(c, right, 0).wait()
        flux_copy(c, left, 1).wait()
        return carry

    lax.fori_loop(0, chunks, arrive, 0)
    to_fold.wait()
    give_from.wait()

    for k, t in enumerate(slots):
        blocks, got = (0, 2), [sides[p // 2, pair_ref[p, t]] for p in (0, 2)]
        if k >= MAXACT - FOLDB:
            blocks, got = blocks + (3,), got + [mirror[...]]
        sums = partial[k] + weigh(t, blocks, got)
        packed_out[k // 2, 96 : 96 + fl, (k % 2) * LANES : (k % 2 + 1) * LANES] = (
            sums[:fl] / sums[fl : fl + 1]
        ).astype(BF16)


def finish(
    from_hbm, hid_in, packed, wocean, mixt,
    hid_hbm, oce_hbm,
    from_ref, oce, from_sem, hid_sem, oce_sem,
):
    tiles, width = oce_hbm.shape[:2]
    get_from = pltpu.make_async_copy(from_hbm, from_ref, from_sem)
    get_from.start()
    keep = pltpu.make_async_copy(hid_in, hid_hbm, hid_sem)
    keep.start()
    oce[MAXACT] = jnp.zeros((width, LANES), BF16)
    for k in range(0, MAXACT, 2):
        base = dot(wocean[...], packed[k // 2]).astype(BF16)
        half = dot(mixt[...], base)
        result = (base.astype(F32) + half + half_gelu(half)).astype(BF16)
        oce[k] = result[:, :LANES]
        oce[k + 1] = result[:, LANES:]

    get_from.wait()
    copies = [pltpu.make_async_copy(oce.at[from_ref[t]], oce_hbm.at[t], oce_sem.at[t]) for t in range(tiles)]
    for copy in copies:
        copy.start()
    for copy in copies:
        copy.wait()
    keep.wait()


def per_device(
    strips,
    atm_in,
    ocean_in,
    lift_weight,
    conv_weight,
    flux_weight,
    ocean_weight,
    couple_weight,
    mix_weight,
    regrid_weight,
    pair_tile,
    ocean_mask,
):
    columns, channels, lat = atm_in.shape
    width = lift_weight.shape[1]
    fl = flux_weight.shape[1]
    tiles, och, cells = ocean_in.shape
    chunks = lat // LANES
    stride = 3 * channels
    depth = -(-9 * channels // 256) * 256
    rows = (columns - 1) * stride + depth
    hbm = pl.BlockSpec(memory_space=pltpu.HBM)
    anywhere = pl.BlockSpec(memory_space=pl.ANY)
    vmem = pl.BlockSpec(memory_space=pltpu.VMEM)
    dma = pltpu.SemaphoreType.DMA
    hidden, *operands, source = pl.pallas_call(
        functools.partial(kernel, strips),
        out_shape=(
            pltpu.VMEM((columns, width, lat), BF16),
            pltpu.VMEM((MAXACT // 2, LANES, 2 * cells), BF16),
            pltpu.VMEM((width, LANES), BF16),
            pltpu.VMEM((width, width), BF16),
            jax.ShapeDtypeStruct((tiles,), jnp.int32),
        ),
        in_specs=[hbm] * 11,
        out_specs=(vmem,) * 4 + (anywhere,),
        scratch_shapes=[
            pltpu.SMEM(pair_tile.shape[::-1], jnp.int32),
            pltpu.SMEM(ocean_mask.shape, jnp.int32),
            pltpu.SMEM(ocean_mask.shape, jnp.int32),
            pltpu.VMEM(lift_weight.shape, BF16),
            pltpu.VMEM(flux_weight.shape[::-1], BF16),
            pltpu.VMEM(ocean_weight.shape, BF16),
            pltpu.VMEM(couple_weight.shape, BF16),
            pltpu.VMEM(mix_weight.shape, BF16),
            pltpu.VMEM((columns + 2, channels, lat), BF16),
            pltpu.VMEM(conv_weight.shape, BF16),
            pltpu.VMEM((och, tiles, cells), BF16),
            pltpu.VMEM(regrid_weight.shape, BF16),
            pltpu.VMEM((chunks, rows, LANES), BF16),
            pltpu.VMEM((depth, width), F32),
            pltpu.VMEM((width, depth), BF16),
            pltpu.VMEM((width, channels), BF16),
            pltpu.VMEM((och * tiles, cells), F32),
            pltpu.VMEM((tiles, LANES, cells), BF16),
            pltpu.VMEM((lat // TLAT, fl, LANES), BF16),
            pltpu.VMEM((2, lat // TLAT, fl, LANES), BF16),
            pltpu.VMEM((fl, LANES), BF16),
            pltpu.VMEM((MAXACT, 2 * fl, LANES), F32),
            dma((11,)),
            dma((2,)),
            dma((2,)),
            dma((2,)),
            dma((chunks, 2)),
            dma((chunks, 2)),
            dma((2,)),
        ],
        compiler_params=pltpu.CompilerParams(
            collective_id=0, has_side_effects=True, vmem_limit_bytes=61 * 1024 * 1024
        ),
        cost_estimate=pl.CostEstimate(
            flops=24 * columns * lat * width * channels, bytes_accessed=8 * 1024 * 1024, transcendentals=1024 * 1024
        ),
    )(
        pair_tile.T, ocean_mask, atm_in, ocean_in.transpose(1, 0, 2), lift_weight, conv_weight,
        flux_weight.T, ocean_weight, couple_weight, mix_weight, regrid_weight,
    )
    return pl.pallas_call(
        finish,
        out_shape=(
            jax.ShapeDtypeStruct((columns, width, lat), BF16),
            jax.ShapeDtypeStruct((tiles, width, cells), BF16),
        ),
        in_specs=[anywhere, anywhere, vmem, vmem, vmem],
        out_specs=(anywhere, anywhere),
        scratch_shapes=[
            pltpu.SMEM((tiles,), jnp.int32),
            pltpu.VMEM((MAXACT + 1, width, cells), BF16),
            dma,
            dma,
            dma((tiles,)),
        ],
        compiler_params=pltpu.CompilerParams(vmem_limit_bytes=61 * 1024 * 1024),
        cost_estimate=pl.CostEstimate(
            flops=2 * MAXACT * cells * width * (width + 128), bytes_accessed=8 * 1024 * 1024, transcendentals=1024 * 1024
        ),
    )(source, hidden, *operands)


def solution(mesh):
    in_specs = (
        P(("groups", "lon"), None, None),
        P(("groups", "lon"), None, None),
        P(),
        P(),
        P(),
        P(),
        P(),
        P(),
        P("lon", None, None, None),
        P("lon", None),
        P("lon"),
    )
    out_specs = (P(("groups", "lon"), None, None), P(("groups", "lon"), None, None))
    return jax.shard_map(
        functools.partial(per_device, mesh.shape["lon"]),
        mesh=mesh,
        in_specs=in_specs,
        out_specs=out_specs,
        check_vma=False,
    )
```

```python
import functools

import jax
import jax.numpy as jnp
from jax import lax
from jax.experimental import pallas as pl
from jax.experimental.pallas import tpu as pltpu
from jax.sharding import PartitionSpec as P

TLAT = 16
FOLDB = 2
MAXACT = 8
LANES = 128
MESH = pl.DeviceIdType.MESH
F32 = jnp.float32
BF16 = jnp.bfloat16


def half_gelu(h):
    return h * jnp.tanh(h * (1.5957691216057308 + 0.285419265090401 * (h * h)))


def dot(a, b):
    return jnp.dot(a, b, preferred_element_type=F32)


def regroup(blocks, tlat):
    count = len(blocks)
    group = lax.broadcasted_iota(jnp.int32, blocks[0].shape, 1) // tlat
    step = count // 2
    while step:
        low = (group // step) % 2 == 0
        out = list(blocks)
        for i in range(count):
            if (i // step) % 2 == 0:
                first, second = blocks[i], blocks[i + step]
                out[i] = jnp.where(low, first, pltpu.roll(second, step * tlat, 1))
                out[i + step] = jnp.where(low, pltpu.roll(first, LANES - step * tlat, 1), second)
        blocks = out
        step //= 2
    return blocks


def water_slots(mask, tiles):
    plain = tiles - FOLDB
    slots = [jnp.int32(0)] * (MAXACT - FOLDB)
    count = jnp.int32(0)
    for t in range(plain):
        wet = mask[t] == 1
        for k in range(min(t + 1, MAXACT - FOLDB)):
            slots[k] = jnp.where(wet & (count == k), t, slots[k])
        count = count + mask[t]
    return slots + [plain + k for k in range(FOLDB)]


def kernel(
    strips,
    pair_hbm, mask_hbm, atm_hbm, ocean_hbm, lift_hbm, conv_hbm, flux_hbm, ow_hbm, cw_hbm, mix_hbm, regrid_hbm,
    hid_out, packed_out, wocean_out, mixt_out, from_out,
    pair_ref, mask_ref, lift_ref, flux_ref, ow_ref, cw_ref, mix_ref, xin, conv_v, ocean_v, regrid_v, col, folded_f, wt, lt, ocean_f, ustate, mine, sides, mirror, partial,
    load_sem, regrid_sem, halo_send, halo_recv, flux_send, flux_recv, mir_sem,
):
    columns, channels, lat = atm_hbm.shape
    width = lift_ref.shape[1]
    och, tiles = ocean_hbm.shape[:2]
    fl = flux_ref.shape[0]
    chunks = lat // LANES
    per = LANES // TLAT
    stride = 3 * channels
    depth = wt.shape[1]

    me = lax.axis_index("lon")
    right = lax.rem(me + 1, strips)
    left = lax.rem(me + strips - 1, strips)
    fold = strips - 1 - me

    def remote(src, dst, send, recv, to):
        return pltpu.make_async_remote_copy(
            src_ref=src, dst_ref=dst, send_sem=send, recv_sem=recv, device_id={"lon": to}, device_id_type=MESH
        )

    barrier = pltpu.get_barrier_semaphore()
    for other in (left, right, fold):
        pl.semaphore_signal(barrier, inc=1, device_id={"lon": other}, device_id_type=MESH)

    load_atm = pltpu.make_async_copy(atm_hbm, xin.at[pl.ds(1, columns)], load_sem.at[0])
    load_conv = pltpu.make_async_copy(conv_hbm, conv_v, load_sem.at[1])
    load_ocean = pltpu.make_async_copy(ocean_hbm, ocean_v, load_sem.at[2])
    load_main = pltpu.make_async_copy(
        regrid_hbm.at[:, pl.ds(0, 3)], regrid_v.at[:, pl.ds(0, 3)], regrid_sem.at[0]
    )
    load_fold = pltpu.make_async_copy(
        regrid_hbm.at[pl.ds(tiles - FOLDB, FOLDB), pl.ds(3, 1)],
        regrid_v.at[pl.ds(tiles - FOLDB, FOLDB), pl.ds(3, 1)],
        regrid_sem.at[1],
    )
    load_ows = [
        pltpu.make_async_copy(source, target, load_sem.at[7 + i])
        for i, (source, target) in enumerate(((ow_hbm, ow_ref), (cw_hbm, cw_ref), (mix_hbm, mix_ref)))
    ]
    smalls = [
        pltpu.make_async_copy(source, target, load_sem.at[3 + i])
        for i, (source, target) in enumerate(
            ((lift_hbm, lift_ref), (flux_hbm, flux_ref), (pair_hbm, pair_ref), (mask_hbm, mask_ref))
        )
    ]
    smalls[0].start()
    load_atm.start()
    load_conv.start()
    for small in smalls[1:]:
        small.start()

    smalls[0].wait()
    lt[...] = lift_ref[...].astype(F32).T.astype(BF16)
    tail = col.shape[1] - (columns + 1) * stride
    for c in range(chunks):
        col[c, (columns + 1) * stride :, :] = jnp.zeros((tail, LANES), BF16)
    folded_f[9 * channels :, :] = jnp.zeros((depth - 9 * channels, width), F32)

    pl.semaphore_wait(barrier, 3)
    halo_r = remote(atm_hbm.at[columns - 1], xin.at[0], halo_send.at[0], halo_recv.at[0], right)
    halo_l = remote(atm_hbm.at[0], xin.at[columns + 1], halo_send.at[1], halo_recv.at[1], left)
    halo_r.start()
    halo_l.start()

    def spread(x):
        v = xin[x].astype(F32)
        lane = lax.broadcasted_iota(jnp.int32, v.shape, 1)
        south = jnp.where(lane == 0, 0.0, pltpu.roll(v, 1, 1))
        north = jnp.where(lane == lat - 1, 0.0, pltpu.roll(v, lat - 1, 1))
        for b, piece in enumerate((south, v, north)):
            piece = piece.astype(BF16)
            at = x * stride + b * channels
            for c in range(chunks):
                col[c, at : at + channels, :] = piece[:, c * LANES : (c + 1) * LANES]

    load_atm.wait()
    load_conv.wait()
    load_ocean.start()
    for load in load_ows:
        load.start()
    load_main.start()
    load_fold.start()
    for small in smalls[1:]:
        small.wait()
    for k in range(9):
        folded_f[k * channels : (k + 1) * channels, :] = dot(lift_ref[...], conv_v[k // 3, k % 3])
        if k < columns:
            spread(k + 1)
    wt[...] = (0.5 * folded_f[...]).T.astype(BF16)

    def flux_copy(c, to, side):
        rows = pl.ds(c * per, per)
        return remote(
            mine.at[rows], sides.at[side, rows], flux_send.at[c, side], flux_recv.at[c, side], to
        )

    to_fold = remote(mine.at[chunks * per - 1], mirror, mir_sem.at[0], mir_sem.at[1], fold)

    def convolve(c, x):
        rhs = jnp.concatenate(
            [col[c, x * stride : x * stride + depth, :], col[c, (x + 1) * stride : (x + 1) * stride + depth, :]],
            axis=1,
        )
        at = (x + 1) * stride + channels
        mid = jnp.concatenate([col[c, at : at + channels, :], col[c, at + stride : at + stride + channels, :]], axis=1)
        return dot(wt[...], rhs), dot(lt[...], mid)

    def activate(c, x, half, lifted):
        hidden = (lifted + half + half_gelu(half)).astype(BF16)
        hid_out[x, :, c * LANES : (c + 1) * LANES] = hidden[:, :LANES]
        hid_out[x + 1, :, c * LANES : (c + 1) * LANES] = hidden[:, LANES:]
        f = dot(flux_ref[...], hidden)
        return [f[:, :LANES], f[:, LANES:]]

    def send(c, flux):
        for a, tile in enumerate(regroup(flux, TLAT)):
            mine[c * per + a] = tile.astype(BF16)
        flux_copy(c, right, 0).start()
        flux_copy(c, left, 1).start()
        if c == chunks - 1:
            to_fold.start()

    def sweep(work):
        ready = convolve(*work[0])
        for i, (c, x) in enumerate(work):
            now = ready
            if i + 1 < len(work):
                ready = convolve(*work[i + 1])
            flux[c, x], flux[c, x + 1] = activate(c, x, *now)
            if x + 2 == columns:
                send(c, [flux.pop((c, k)) for k in range(columns)])

    flux = {}
    bands = list(reversed(range(chunks)))
    sweep([(c, x) for c in bands for x in range(2, columns - 2, 2)])
    halo_r.wait()
    halo_l.wait()
    spread(0)
    spread(columns + 1)

    sweep([(c, x) for c in bands for x in (0, columns - 2)])

    load_ocean.wait()
    ocean_f[...] = ocean_v[...].astype(F32).reshape(ocean_f.shape)
    for t in range(tiles):
        ustate[t, 80:, :] = jnp.zeros((ustate.shape[1] - 80, LANES), BF16)
        ustate[t, 0:och, :] = ocean_f[pl.ds(t, och, stride=tiles), :].astype(BF16)

    slots = water_slots(mask_ref, tiles)
    ahead = jnp.int32(0)
    lane = lax.broadcasted_iota(jnp.int32, from_out.shape, 1)
    origin = jnp.full(from_out.shape, MAXACT, jnp.int32)
    for t in range(tiles):
        slot = ahead if t < tiles - FOLDB else jnp.int32(MAXACT - tiles + t)
        origin = jnp.where(lane == t, jnp.where(mask_ref[t] == 1, slot, MAXACT), origin)
        ahead = ahead + mask_ref[t]
    from_out[...] = origin
    for k, t in enumerate(slots):
        packed_out[k // 2, :, (k % 2) * LANES : (k % 2 + 1) * LANES] = ustate[t]

    for load in load_ows:
        load.wait()
    mixt_out[...] = (0.5 * mix_ref[...].astype(F32)).T.astype(BF16)
    joined = jnp.concatenate(
        [
            ow_ref[...].astype(F32),
            jnp.zeros((96 - och, width), F32),
            cw_ref[...].astype(F32),
            jnp.zeros((LANES - 96 - fl, width), F32),
        ],
        axis=0,
    )
    wocean_out[...] = joined.T.astype(BF16)

    load_main.wait()
    load_fold.wait()
    ones = jnp.ones((fl, LANES), BF16)

    def weigh(t, blocks, got):
        lhs = jnp.concatenate([jnp.concatenate([g, ones], axis=0) for g in got], axis=1)
        rhs = jnp.concatenate([regrid_v[t, p] for p in blocks], axis=1)
        return lax.dot_general(lhs, rhs, (((1,), (1,)), ((), ())), preferred_element_type=F32)

    for k, t in enumerate(slots):
        partial[k] = weigh(t, (1,), [mine[pair_ref[1, t]]])

    def arrive(c, carry):
        flux_copy(c, right, 0).wait()
        flux_copy(c, left, 1).wait()
        return carry

    lax.fori_loop(0, chunks, arrive, 0)
    to_fold.wait()

    for k, t in enumerate(slots):
        blocks, got = (0, 2), [sides[p // 2, pair_ref[p, t]] for p in (0, 2)]
        if k >= MAXACT - FOLDB:
            blocks, got = blocks + (3,), got + [mirror[...]]
        sums = partial[k] + weigh(t, blocks, got)
        packed_out[k // 2, 96 : 96 + fl, (k % 2) * LANES : (k % 2 + 1) * LANES] = (
            sums[:fl] / sums[fl : fl + 1]
        ).astype(BF16)


def finish(
    from_in, hid_in, packed, wocean, mixt,
    hid_hbm, oce_hbm,
    oce, hid_sem, oce_sem,
):
    tiles, width = oce_hbm.shape[:2]
    keep = pltpu.make_async_copy(hid_in, hid_hbm, hid_sem)
    keep.start()
    oce[MAXACT] = jnp.zeros((width, LANES), BF16)
    for k in range(0, MAXACT, 2):
        base = dot(wocean[...], packed[k // 2]).astype(BF16)
        half = dot(mixt[...], base)
        result = (base.astype(F32) + half + half_gelu(half)).astype(BF16)
        oce[k] = result[:, :LANES]
        oce[k + 1] = result[:, LANES:]

    origin = from_in[...]
    copies = [pltpu.make_async_copy(oce.at[origin[0, t]], oce_hbm.at[t], oce_sem.at[t]) for t in range(tiles)]
    for copy in copies:
        copy.start()
    for copy in copies:
        copy.wait()
    keep.wait()


def per_device(
    strips,
    atm_in,
    ocean_in,
    lift_weight,
    conv_weight,
    flux_weight,
    ocean_weight,
    couple_weight,
    mix_weight,
    regrid_weight,
    pair_tile,
    ocean_mask,
):
    columns, channels, lat = atm_in.shape
    width = lift_weight.shape[1]
    fl = flux_weight.shape[1]
    tiles, och, cells = ocean_in.shape
    chunks = lat // LANES
    stride = 3 * channels
    depth = -(-9 * channels // 256) * 256
    rows = (columns - 1) * stride + depth
    hbm = pl.BlockSpec(memory_space=pltpu.HBM)
    anywhere = pl.BlockSpec(memory_space=pl.ANY)
    vmem = pl.BlockSpec(memory_space=pltpu.VMEM)
    dma = pltpu.SemaphoreType.DMA
    hidden, *operands, source = pl.pallas_call(
        functools.partial(kernel, strips),
        out_shape=(
            pltpu.VMEM((columns, width, lat), BF16),
            pltpu.VMEM((MAXACT // 2, LANES, 2 * cells), BF16),
            pltpu.VMEM((width, LANES), BF16),
            pltpu.VMEM((width, width), BF16),
            pltpu.VMEM((8, LANES), jnp.int32),
        ),
        in_specs=[hbm] * 11,
        out_specs=(vmem,) * 5,
        scratch_shapes=[
            pltpu.SMEM(pair_tile.shape[::-1], jnp.int32),
            pltpu.SMEM(ocean_mask.shape, jnp.int32),
            pltpu.VMEM(lift_weight.shape, BF16),
            pltpu.VMEM(flux_weight.shape[::-1], BF16),
            pltpu.VMEM(ocean_weight.shape, BF16),
            pltpu.VMEM(couple_weight.shape, BF16),
            pltpu.VMEM(mix_weight.shape, BF16),
            pltpu.VMEM((columns + 2, channels, lat), BF16),
            pltpu.VMEM(conv_weight.shape, BF16),
            pltpu.VMEM((och, tiles, cells), BF16),
            pltpu.VMEM(regrid_weight.shape, BF16),
            pltpu.VMEM((chunks, rows, LANES), BF16),
            pltpu.VMEM((depth, width), F32),
            pltpu.VMEM((width, depth), BF16),
            pltpu.VMEM((width, channels), BF16),
            pltpu.VMEM((och * tiles, cells), F32),
            pltpu.VMEM((tiles, LANES, cells), BF16),
            pltpu.VMEM((lat // TLAT, fl, LANES), BF16),
            pltpu.VMEM((2, lat // TLAT, fl, LANES), BF16),
            pltpu.VMEM((fl, LANES), BF16),
            pltpu.VMEM((MAXACT, 2 * fl, LANES), F32),
            dma((10,)),
            dma((2,)),
            dma((2,)),
            dma((2,)),
            dma((chunks, 2)),
            dma((chunks, 2)),
            dma((2,)),
        ],
        compiler_params=pltpu.CompilerParams(
            collective_id=0, has_side_effects=True, vmem_limit_bytes=62432 * 1024
        ),
        cost_estimate=pl.CostEstimate(
            flops=24 * columns * lat * width * channels, bytes_accessed=8 * 1024 * 1024, transcendentals=1024 * 1024
        ),
    )(
        pair_tile.T, ocean_mask, atm_in, ocean_in.transpose(1, 0, 2), lift_weight, conv_weight,
        flux_weight.T, ocean_weight, couple_weight, mix_weight, regrid_weight,
    )
    return pl.pallas_call(
        finish,
        out_shape=(
            jax.ShapeDtypeStruct((columns, width, lat), BF16),
            jax.ShapeDtypeStruct((tiles, width, cells), BF16),
        ),
        in_specs=[vmem, anywhere, vmem, vmem, vmem],
        out_specs=(anywhere, anywhere),
        scratch_shapes=[
            pltpu.VMEM((MAXACT + 1, width, cells), BF16),
            dma,
            dma((tiles,)),
        ],
        compiler_params=pltpu.CompilerParams(vmem_limit_bytes=50 * 1024 * 1024),
        cost_estimate=pl.CostEstimate(
            flops=2 * MAXACT * cells * width * (width + 128), bytes_accessed=8 * 1024 * 1024, transcendentals=1024 * 1024
        ),
    )(source, hidden, *operands)


def solution(mesh):
    in_specs = (
        P(("groups", "lon"), None, None),
        P(("groups", "lon"), None, None),
        P(),
        P(),
        P(),
        P(),
        P(),
        P(),
        P("lon", None, None, None),
        P("lon", None),
        P("lon"),
    )
    out_specs = (P(("groups", "lon"), None, None), P(("groups", "lon"), None, None))
    return jax.shard_map(
        functools.partial(per_device, mesh.shape["lon"]),
        mesh=mesh,
        in_specs=in_specs,
        out_specs=out_specs,
        check_vma=False,
    )
```

```python
import functools

import jax
import jax.numpy as jnp
from jax import lax
from jax.experimental import pallas as pl
from jax.experimental.pallas import tpu as pltpu
from jax.sharding import PartitionSpec as P

TLAT = 16
FOLDB = 2
MAXACT = 8
LANES = 128
MESH = pl.DeviceIdType.MESH
F32 = jnp.float32
BF16 = jnp.bfloat16


def half_gelu(h):
    return h * jnp.tanh(h * (1.5957691216057308 + 0.285419265090401 * (h * h)))


def dot(a, b):
    return jnp.dot(a, b, preferred_element_type=F32)


def regroup(blocks, tlat):
    count = len(blocks)
    group = lax.broadcasted_iota(jnp.int32, blocks[0].shape, 1) // tlat
    step = count // 2
    while step:
        low = (group // step) % 2 == 0
        out = list(blocks)
        for i in range(count):
            if (i // step) % 2 == 0:
                first, second = blocks[i], blocks[i + step]
                out[i] = jnp.where(low, first, pltpu.roll(second, step * tlat, 1))
                out[i + step] = jnp.where(low, pltpu.roll(first, LANES - step * tlat, 1), second)
        blocks = out
        step //= 2
    return blocks


def water_slots(mask, tiles):
    plain = tiles - FOLDB
    slots = [jnp.int32(0)] * (MAXACT - FOLDB)
    count = jnp.int32(0)
    for t in range(plain):
        wet = mask[t] == 1
        for k in range(min(t + 1, MAXACT - FOLDB)):
            slots[k] = jnp.where(wet & (count == k), t, slots[k])
        count = count + mask[t]
    return slots + [plain + k for k in range(FOLDB)]


def kernel(
    strips,
    pair_hbm, mask_hbm, atm_hbm, ocean_hbm, lift_hbm, conv_hbm, flux_hbm, ow_hbm, cw_hbm, mix_hbm, regrid_hbm,
    hid_out, packed_out, wocean_out, mixt_out, from_out,
    pair_ref, mask_ref, lift_ref, flux_ref, ow_ref, cw_ref, mix_ref, xin, conv_v, ocean_v, regrid_v, col, folded_f, wt, lt, ocean_f, ustate, mine, sides, mirror, partial,
    load_sem, conv_sem, regrid_sem, halo_send, halo_recv, flux_send, flux_recv, mir_sem,
):
    columns, channels, lat = atm_hbm.shape
    width = lift_ref.shape[1]
    och, tiles = ocean_hbm.shape[:2]
    fl = flux_ref.shape[0]
    chunks = lat // LANES
    per = LANES // TLAT
    stride = 3 * channels
    depth = wt.shape[1]

    me = lax.axis_index("lon")
    right = lax.rem(me + 1, strips)
    left = lax.rem(me + strips - 1, strips)
    fold = strips - 1 - me

    def remote(src, dst, send, recv, to):
        return pltpu.make_async_remote_copy(
            src_ref=src, dst_ref=dst, send_sem=send, recv_sem=recv, device_id={"lon": to}, device_id_type=MESH
        )

    barrier = pltpu.get_barrier_semaphore()
    for other in (left, right, fold):
        pl.semaphore_signal(barrier, inc=1, device_id={"lon": other}, device_id_type=MESH)

    load_atm = pltpu.make_async_copy(atm_hbm, xin.at[pl.ds(1, columns)], load_sem.at[0])
    load_conv = [
        pltpu.make_async_copy(conv_hbm.at[k // 3, k % 3], conv_v.at[k // 3, k % 3], conv_sem.at[k]) for k in range(9)
    ]
    load_ocean = pltpu.make_async_copy(ocean_hbm, ocean_v, load_sem.at[2])
    load_main = pltpu.make_async_copy(
        regrid_hbm.at[:, pl.ds(0, 3)], regrid_v.at[:, pl.ds(0, 3)], regrid_sem.at[0]
    )
    load_fold = pltpu.make_async_copy(
        regrid_hbm.at[pl.ds(tiles - FOLDB, FOLDB), pl.ds(3, 1)],
        regrid_v.at[pl.ds(tiles - FOLDB, FOLDB), pl.ds(3, 1)],
        regrid_sem.at[1],
    )
    load_ows = [
        pltpu.make_async_copy(source, target, load_sem.at[7 + i])
        for i, (source, target) in enumerate(((ow_hbm, ow_ref), (cw_hbm, cw_ref), (mix_hbm, mix_ref)))
    ]
    smalls = [
        pltpu.make_async_copy(source, target, load_sem.at[3 + i])
        for i, (source, target) in enumerate(
            ((lift_hbm, lift_ref), (flux_hbm, flux_ref), (pair_hbm, pair_ref), (mask_hbm, mask_ref))
        )
    ]
    smalls[0].start()
    load_atm.start()
    for load in load_conv:
        load.start()
    for small in smalls[1:]:
        small.start()

    smalls[0].wait()
    lt[...] = lift_ref[...].astype(F32).T.astype(BF16)
    tail = col.shape[1] - (columns + 1) * stride
    for c in range(chunks):
        col[c, (columns + 1) * stride :, :] = jnp.zeros((tail, LANES), BF16)
    folded_f[9 * channels :, :] = jnp.zeros((depth - 9 * channels, width), F32)

    pl.semaphore_wait(barrier, 3)
    halo_r = remote(atm_hbm.at[columns - 1], xin.at[0], halo_send.at[0], halo_recv.at[0], right)
    halo_l = remote(atm_hbm.at[0], xin.at[columns + 1], halo_send.at[1], halo_recv.at[1], left)
    halo_r.start()
    halo_l.start()

    def spread(x):
        v = xin[x].astype(F32)
        lane = lax.broadcasted_iota(jnp.int32, v.shape, 1)
        south = jnp.where(lane == 0, 0.0, pltpu.roll(v, 1, 1))
        north = jnp.where(lane == lat - 1, 0.0, pltpu.roll(v, lat - 1, 1))
        for b, piece in enumerate((south, v, north)):
            piece = piece.astype(BF16)
            at = x * stride + b * channels
            for c in range(chunks):
                col[c, at : at + channels, :] = piece[:, c * LANES : (c + 1) * LANES]

    load_atm.wait()
    load_ocean.start()
    for load in load_ows:
        load.start()
    load_main.start()
    load_fold.start()
    for small in smalls[1:]:
        small.wait()
    for k in range(9):
        if k % 3 == 0:
            for load in load_conv[k : k + 3]:
                load.wait()
        folded_f[k * channels : (k + 1) * channels, :] = dot(lift_ref[...], conv_v[k // 3, k % 3])
        if k < columns:
            spread(k + 1)
    wt[...] = (0.5 * folded_f[...]).T.astype(BF16)

    def flux_copy(c, to, side):
        rows = pl.ds(c * per, per)
        return remote(
            mine.at[rows], sides.at[side, rows], flux_send.at[c, side], flux_recv.at[c, side], to
        )

    to_fold = remote(mine.at[chunks * per - 1], mirror, mir_sem.at[0], mir_sem.at[1], fold)

    def convolve(c, x):
        rhs = jnp.concatenate(
            [col[c, x * stride : x * stride + depth, :], col[c, (x + 1) * stride : (x + 1) * stride + depth, :]],
            axis=1,
        )
        at = (x + 1) * stride + channels
        mid = jnp.concatenate([col[c, at : at + channels, :], col[c, at + stride : at + stride + channels, :]], axis=1)
        return dot(wt[...], rhs), dot(lt[...], mid)

    def activate(c, x, half, lifted):
        hidden = (lifted + half + half_gelu(half)).astype(BF16)
        hid_out[x, :, c * LANES : (c + 1) * LANES] = hidden[:, :LANES]
        hid_out[x + 1, :, c * LANES : (c + 1) * LANES] = hidden[:, LANES:]
        f = dot(flux_ref[...], hidden)
        return [f[:, :LANES], f[:, LANES:]]

    def send(c, flux):
        for a, tile in enumerate(regroup(flux, TLAT)):
            mine[c * per + a] = tile.astype(BF16)
        flux_copy(c, right, 0).start()
        flux_copy(c, left, 1).start()
        if c == chunks - 1:
            to_fold.start()

    def sweep(work):
        ready = convolve(*work[0])
        for i, (c, x) in enumerate(work):
            now = ready
            if i + 1 < len(work):
                ready = convolve(*work[i + 1])
            flux[c, x], flux[c, x + 1] = activate(c, x, *now)
            if x + 2 == columns:
                send(c, [flux.pop((c, k)) for k in range(columns)])

    flux = {}
    bands = list(reversed(range(chunks)))
    sweep([(c, x) for c in bands for x in range(2, columns - 2, 2)])
    halo_r.wait_recv()
    halo_l.wait_recv()
    spread(0)
    spread(columns + 1)

    sweep([(c, x) for c in bands for x in (0, columns - 2)])

    load_ocean.wait()
    ocean_f[...] = ocean_v[...].astype(F32).reshape(ocean_f.shape)
    for t in range(tiles):
        ustate[t, 80:, :] = jnp.zeros((ustate.shape[1] - 80, LANES), BF16)
        ustate[t, 0:och, :] = ocean_f[pl.ds(t, och, stride=tiles), :].astype(BF16)

    slots = water_slots(mask_ref, tiles)
    ahead = jnp.int32(0)
    lane = lax.broadcasted_iota(jnp.int32, from_out.shape, 1)
    origin = jnp.full(from_out.shape, MAXACT, jnp.int32)
    for t in range(tiles):
        slot = ahead if t < tiles - FOLDB else jnp.int32(MAXACT - tiles + t)
        origin = jnp.where(lane == t, jnp.where(mask_ref[t] == 1, slot, MAXACT), origin)
        ahead = ahead + mask_ref[t]
    from_out[...] = origin
    for k, t in enumerate(slots):
        packed_out[k // 2, :, (k % 2) * LANES : (k % 2 + 1) * LANES] = ustate[t]

    for load in load_ows:
        load.wait()
    mixt_out[...] = (0.5 * mix_ref[...].astype(F32)).T.astype(BF16)
    joined = jnp.concatenate(
        [
            ow_ref[...].astype(F32),
            jnp.zeros((96 - och, width), F32),
            cw_ref[...].astype(F32),
            jnp.zeros((LANES - 96 - fl, width), F32),
        ],
        axis=0,
    )
    wocean_out[...] = joined.T.astype(BF16)

    load_main.wait()
    load_fold.wait()
    ones = jnp.ones((fl, LANES), BF16)

    def weigh(t, blocks, got):
        lhs = jnp.concatenate([jnp.concatenate([g, ones], axis=0) for g in got], axis=1)
        rhs = jnp.concatenate([regrid_v[t, p] for p in blocks], axis=1)
        return lax.dot_general(lhs, rhs, (((1,), (1,)), ((), ())), preferred_element_type=F32)

    for k, t in enumerate(slots):
        partial[k] = weigh(t, (1,), [mine[pair_ref[1, t]]])

    def arrive(c, carry):
        flux_copy(c, right, 0).wait_recv()
        flux_copy(c, left, 1).wait_recv()
        return carry

    lax.fori_loop(0, chunks, arrive, 0)
    to_fold.wait_recv()

    for k, t in enumerate(slots):
        blocks, got = (0, 2), [sides[p // 2, pair_ref[p, t]] for p in (0, 2)]
        if k >= MAXACT - FOLDB:
            blocks, got = blocks + (3,), got + [mirror[...]]
        sums = partial[k] + weigh(t, blocks, got)
        packed_out[k // 2, 96 : 96 + fl, (k % 2) * LANES : (k % 2 + 1) * LANES] = (
            sums[:fl] / sums[fl : fl + 1]
        ).astype(BF16)

    def leave(c, carry):
        flux_copy(c, right, 0).wait_send()
        flux_copy(c, left, 1).wait_send()
        return carry

    lax.fori_loop(0, chunks, leave, 0)
    to_fold.wait_send()
    for halo in (halo_r, halo_l):
        halo.wait_send()


def finish(
    from_in, hid_in, packed, wocean, mixt,
    hid_hbm, oce_hbm,
    oce, hid_sem, oce_sem,
):
    tiles, width = oce_hbm.shape[:2]
    keeps = [pltpu.make_async_copy(hid_in.at[x], hid_hbm.at[x], hid_sem.at[x]) for x in range(hid_in.shape[0])]
    for keep in keeps:
        keep.start()
    oce[MAXACT] = jnp.zeros((width, LANES), BF16)
    for k in range(0, MAXACT, 2):
        base = dot(wocean[...], packed[k // 2]).astype(BF16)
        half = dot(mixt[...], base)
        result = (base.astype(F32) + half + half_gelu(half)).astype(BF16)
        oce[k] = result[:, :LANES]
        oce[k + 1] = result[:, LANES:]

    origin = from_in[...]
    copies = [pltpu.make_async_copy(oce.at[origin[0, t]], oce_hbm.at[t], oce_sem.at[t]) for t in range(tiles)]
    for copy in copies:
        copy.start()
    for copy in copies:
        copy.wait()
    for keep in keeps:
        keep.wait()


def per_device(
    strips,
    atm_in,
    ocean_in,
    lift_weight,
    conv_weight,
    flux_weight,
    ocean_weight,
    couple_weight,
    mix_weight,
    regrid_weight,
    pair_tile,
    ocean_mask,
):
    columns, channels, lat = atm_in.shape
    width = lift_weight.shape[1]
    fl = flux_weight.shape[1]
    tiles, och, cells = ocean_in.shape
    chunks = lat // LANES
    stride = 3 * channels
    depth = -(-9 * channels // 256) * 256
    rows = (columns - 1) * stride + depth
    hbm = pl.BlockSpec(memory_space=pltpu.HBM)
    anywhere = pl.BlockSpec(memory_space=pl.ANY)
    vmem = pl.BlockSpec(memory_space=pltpu.VMEM)
    dma = pltpu.SemaphoreType.DMA
    hidden, *operands, source = pl.pallas_call(
        functools.partial(kernel, strips),
        out_shape=(
            pltpu.VMEM((columns, width, lat), BF16),
            pltpu.VMEM((MAXACT // 2, LANES, 2 * cells), BF16),
            pltpu.VMEM((width, LANES), BF16),
            pltpu.VMEM((width, width), BF16),
            pltpu.VMEM((8, LANES), jnp.int32),
        ),
        in_specs=[hbm] * 11,
        out_specs=(vmem,) * 5,
        scratch_shapes=[
            pltpu.SMEM(pair_tile.shape[::-1], jnp.int32),
            pltpu.SMEM(ocean_mask.shape, jnp.int32),
            pltpu.VMEM(lift_weight.shape, BF16),
            pltpu.VMEM(flux_weight.shape[::-1], BF16),
            pltpu.VMEM(ocean_weight.shape, BF16),
            pltpu.VMEM(couple_weight.shape, BF16),
            pltpu.VMEM(mix_weight.shape, BF16),
            pltpu.VMEM((columns + 2, channels, lat), BF16),
            pltpu.VMEM(conv_weight.shape, BF16),
            pltpu.VMEM((och, tiles, cells), BF16),
            pltpu.VMEM(regrid_weight.shape, BF16),
            pltpu.VMEM((chunks, rows, LANES), BF16),
            pltpu.VMEM((depth, width), F32),
            pltpu.VMEM((width, depth), BF16),
            pltpu.VMEM((width, channels), BF16),
            pltpu.VMEM((och * tiles, cells), F32),
            pltpu.VMEM((tiles, LANES, cells), BF16),
            pltpu.VMEM((lat // TLAT, fl, LANES), BF16),
            pltpu.VMEM((2, lat // TLAT, fl, LANES), BF16),
            pltpu.VMEM((fl, LANES), BF16),
            pltpu.VMEM((MAXACT, 2 * fl, LANES), F32),
            dma((10,)),
            dma((9,)),
            dma((2,)),
            dma((2,)),
            dma((2,)),
            dma((chunks, 2)),
            dma((chunks, 2)),
            dma((2,)),
        ],
        compiler_params=pltpu.CompilerParams(
            collective_id=0, has_side_effects=True, vmem_limit_bytes=62432 * 1024
        ),
        cost_estimate=pl.CostEstimate(
            flops=24 * columns * lat * width * channels, bytes_accessed=8 * 1024 * 1024, transcendentals=1024 * 1024
        ),
    )(
        pair_tile.T, ocean_mask, atm_in, ocean_in.transpose(1, 0, 2), lift_weight, conv_weight,
        flux_weight.T, ocean_weight, couple_weight, mix_weight, regrid_weight,
    )
    return pl.pallas_call(
        finish,
        out_shape=(
            jax.ShapeDtypeStruct((columns, width, lat), BF16),
            jax.ShapeDtypeStruct((tiles, width, cells), BF16),
        ),
        in_specs=[vmem, anywhere, vmem, vmem, vmem],
        out_specs=(anywhere, anywhere),
        scratch_shapes=[
            pltpu.VMEM((MAXACT + 1, width, cells), BF16),
            dma((columns,)),
            dma((tiles,)),
        ],
        compiler_params=pltpu.CompilerParams(vmem_limit_bytes=50 * 1024 * 1024),
        cost_estimate=pl.CostEstimate(
            flops=2 * MAXACT * cells * width * (width + 128), bytes_accessed=8 * 1024 * 1024, transcendentals=1024 * 1024
        ),
    )(source, hidden, *operands)


def solution(mesh):
    in_specs = (
        P(("groups", "lon"), None, None),
        P(("groups", "lon"), None, None),
        P(),
        P(),
        P(),
        P(),
        P(),
        P(),
        P("lon", None, None, None),
        P("lon", None),
        P("lon"),
    )
    out_specs = (P(("groups", "lon"), None, None), P(("groups", "lon"), None, None))
    return jax.shard_map(
        functools.partial(per_device, mesh.shape["lon"]),
        mesh=mesh,
        in_specs=in_specs,
        out_specs=out_specs,
        check_vma=False,
    )
```
